512 devices in a mesh: seq: 128 (over z, x, core), head: 4 (over y).
Axes of the slice: x: 4, y: 4, z: 16, core: 2. Of those that a mesh axis runs over, the one named last changes fastest.
Arguments:
- tokens: bfloat16 [16384, 1024], P('seq', 'head'), may hold values from -6 to 6
- key_weight: bfloat16 [1024, 1024], P(None, 'head'), may hold values from -0.1875 to 0.1875
- value_weight: bfloat16 [1024, 1024], P(None, 'head'), may hold values from -0.1875 to 0.1875
- buckets: int32 [4, 16, 16384, 1], P(None, 'head', 'seq'), may hold values from 0 to 127; in each aligned block of 128 rows (0 to 127, 128 to 255, ..., all dimensions but the last counted through in order) at most 2 rows name the same one
- cotangent: bfloat16 [16384, 1024], P('seq', 'head'), may hold values from -6 to 6
Outputs:
- attention: float32 [16384, 1024], P('seq', 'head')
- grad_input: float32 [16384, 1024], P('seq', 'head')
The draws below stay inside these ranges and needn't reach their ends.
Inputs may be any that keep to these rules, and one draw needn't show every extreme that they name: `buckets`: in each round and head, at most 2 of the 128 tokens of one device share a bucket, and this many do in some of them.
All inputs are finite; a program needn't handle non-finite values.
Results may differ from the reference program's by a relative error of at most 0.017.
Values may be sent and summed in bfloat16 or wider, within the bound.
A program may use at most 64 MiB of HBM per device.

```python
import math
import jax
import jax.numpy as jnp
import numpy as np
from jax import lax

HEADS = 16
HEAD_SIZE = 64
ROUNDS = 4
TOK_DEV = 128
D = 1024
TOKENS = 16384
NBUCKETS = 128
BMOST = 2
N_SEQ = 128


def levels(own_key, dims, shards, smallest, high):
    level = 1.0
    for dim, blocks in shards:
        draws = jax.random.uniform(jax.random.fold_in(jax.random.fold_in(own_key, 6), dim), (blocks,), jnp.float32, smallest / len(shards), high / len(shards))
        level = level * jnp.repeat(jnp.exp(draws), dims[dim] // blocks).reshape((-1,) + (1,) * (len(dims) - 1 - dim))
    return level


def routed_block(stream_key, own, number, rows, count, top, reach, lean):
    sequence = jax.random.permutation(stream_key, count)
    crowded, common = load_shares(count, rows * top, reach, lean, True), load_shares(count, rows * top, reach, lean, False)
    places = jnp.arange(count)

    def named(tallies, rotation):
        used = int((tallies > 0).sum())
        fixed = max(1, used // 4)
        shifted = fixed + (places - fixed + rotation * (used - fixed)) % max(1, count - fixed)
        return jnp.zeros((count,), jnp.int32).at[sequence[jnp.where(places < fixed, places, shifted)]].set(jnp.asarray(tallies, jnp.int32))

    tallies = jnp.where(number % 4 == 0, named(crowded, number // 4), named(common, number - number // 4 - 1))
    mixed = jax.random.permutation(jax.random.fold_in(own, 3), count)
    giver, taker = mixed[0:count // 2 * 2:2], mixed[1:count // 2 * 2:2]
    slack = jnp.minimum(tallies[giver] - 1, reach - tallies[taker]) // 2
    slack = jnp.where((giver == sequence[0]) | (taker == sequence[0]) | (tallies[taker] == 0), 0, jnp.maximum(slack, 0))
    shifted = jax.random.randint(jax.random.fold_in(own, 4), (count // 2,), 0, 1 << 20) % (slack + 1)
    tallies = tallies.at[giver].add(-shifted).at[taker].add(shifted)
    members = jnp.searchsorted(jnp.cumsum(tallies), jnp.arange(rows * top), side="right").astype(jnp.int32)
    grid = members.reshape(top, rows).T
    grid = grid[jax.random.permutation(jax.random.fold_in(own, 1), rows)]
    rotation = jax.random.randint(jax.random.fold_in(own, 2), (rows, 1), 0, top)
    return jnp.take_along_axis(grid, (jnp.arange(top)[None, :] + rotation) % top, axis=1)


def load_shares(count, total, most, lean, full):
    weights = [(1 << 20) // math.isqrt(rank ** lean) + 1 for rank in range(1, count + 1)]
    largest = most if full else min(most, max(-(-total // count), total * weights[0] // sum(weights)))
    least = 1 if total - largest >= count - 1 else 0
    given, rest = [largest] + [least] * (count - 1), total - largest - least * (count - 1)
    while rest > 0:
        movable = [i for i in range(1, count) if given[i] < largest] or [i for i in range(1, count) if given[i] < most]
        pool, remaining = sum([weights[i] for i in movable]), rest
        for i in movable:
            addition = min(most - given[i], max(1, remaining * weights[i] // pool), rest)
            given[i] = given[i] + addition
            rest = rest - addition
    return np.array(given)


def centred(own_key, shape, width, reach, pieces=(), kind=jnp.bfloat16):
    entries = jax.random.normal(own_key, shape, jnp.float32) * width
    if len(pieces) > 0:
        entries = levels(own_key, shape, pieces, -0.22, 0.18) * entries
    return jnp.clip(entries, min=-reach, max=reach).astype(kind)


def setup_inputs(seed: int = 0) -> dict:
    splits = jax.random.split(jax.random.key(seed), 6)
    tokens = centred(splits[0], (TOKENS, D), 1.0, 6.0, ((0, 128), (1, 4)))
    key_weight = centred(splits[1], (D, D), D ** -0.5, 0.1875, ((1, 4),))
    value_weight = centred(splits[2], (D, D), D ** -0.5, 0.1875, ((1, 4),))
    buckets_keys = jax.random.split(jax.random.fold_in(splits[3], 1), ROUNDS * HEADS * TOKENS // TOK_DEV)
    buckets_turns = jax.random.permutation(jax.random.fold_in(splits[3], 3), ROUNDS * HEADS * TOKENS // TOK_DEV)
    buckets = jax.vmap(lambda own, number: routed_block(jax.random.fold_in(splits[3], 2), own, number, TOK_DEV, NBUCKETS, 1, BMOST, 2))(buckets_keys, buckets_turns).reshape((ROUNDS, HEADS, TOKENS, 1))
    cotangent = centred(splits[4], (TOKENS, D), 1.0, 6.0, ((0, 128), (1, 4)))
    return {"tokens": tokens, "key_weight": key_weight, "value_weight": value_weight, "buckets": buckets, "cotangent": cotangent}


sharpness = 16.0

def unit_rows(rows):
    rows_f = rows.astype(jnp.float32)
    length = jnp.sqrt(lax.optimization_barrier(jnp.sum(rows_f * rows_f, axis=-1, keepdims=True)) + 1e-06)
    unit = rows_f / length
    return (unit, unit.astype(jnp.bfloat16), length)

def bucket_probs(unit_b, valid):
    capacity = unit_b.shape[1]
    unit_f = unit_b.astype(jnp.float32)
    scores = sharpness * jnp.einsum('bie,bje->bij', unit_f, unit_f)
    diagonal = jnp.arange(capacity)[:, None] == jnp.arange(capacity)[None, :]
    weights = jnp.where(diagonal[None], 1.0, jnp.exp(scores) * valid[:, None, :])
    totals = lax.optimization_barrier(jnp.sum(weights, axis=-1))
    return (weights / totals[..., None], totals, diagonal)

def arrange(bucket_ids):
    capacity = N_SEQ * BMOST
    order = jnp.argsort(bucket_ids, stable=True).astype(jnp.int32)
    counts = lax.optimization_barrier(jnp.sum((bucket_ids[None, :] == jnp.arange(N_SEQ, dtype=jnp.int32)[:, None]).astype(jnp.int32), axis=1))
    starts = jnp.cumsum(counts) - counts
    places = jnp.arange(capacity, dtype=jnp.int32)
    position = starts[:, None] + places[None, :]
    index_rows = order[jnp.clip(position, 0, TOKENS - 1)]
    valid = (places[None, :] < counts[:, None]).astype(jnp.float32)
    inverse = jnp.zeros((TOKENS,), jnp.int32).at[order].set(jnp.arange(TOKENS, dtype=jnp.int32))
    flat = bucket_ids * capacity + (inverse - starts[bucket_ids])
    return (index_rows, valid, flat.astype(jnp.int32))

def in_buckets(rows, index_rows, valid):
    picked = rows[index_rows]
    return jnp.where(valid.reshape(valid.shape + (1,) * (picked.ndim - 2)) > 0, picked, jnp.zeros_like(picked))

def to_tokens(bucketed, flat):
    return bucketed.reshape((-1,) + bucketed.shape[2:])[flat]

def head_pass(inputs):
    shared_rows, value_rows, head_ids, head_cot = inputs
    layouts = []
    outputs = []
    log_totals = []
    for turn in range(ROUNDS):
        index_rows, valid, flat = arrange(head_ids[turn])
        layouts.append((index_rows, valid, flat))
        shared_b = in_buckets(shared_rows, index_rows, valid)
        value_b = in_buckets(value_rows, index_rows, valid)
        unit, unit_b, length = unit_rows(shared_b)
        probs, totals, diagonal = bucket_probs(unit_b, valid)
        result = jnp.einsum('bij,bje->bie', probs.astype(jnp.bfloat16).astype(jnp.float32), value_b.astype(jnp.float32))
        outputs.append(to_tokens(result, flat))
        log_totals.append(to_tokens(jnp.log(totals), flat))
    stacked_lse = jnp.stack(log_totals)
    combined = jnp.log(lax.optimization_barrier(jnp.sum(jnp.exp(stacked_lse), axis=0)))
    share = jnp.exp(stacked_lse - combined[None])
    attention = lax.optimization_barrier(jnp.sum(share[..., None] * jnp.stack(outputs), axis=0))
    cot_f = head_cot.astype(jnp.float32)
    along = lax.optimization_barrier(jnp.sum(cot_f * attention, axis=-1))
    grad_shared = jnp.zeros(shared_rows.shape, jnp.float32)
    grad_values = jnp.zeros(value_rows.shape, jnp.float32)
    for turn in range(ROUNDS):
        index_rows, valid, flat = layouts[turn]
        grad_round = share[turn][:, None] * cot_f
        offsets = -share[turn] * along
        shared_b = in_buckets(shared_rows, index_rows, valid)
        value_b = in_buckets(value_rows, index_rows, valid)
        grad_b = in_buckets(grad_round, index_rows, valid).astype(jnp.bfloat16)
        offset_b = in_buckets(offsets, index_rows, valid)
        unit, unit_b, length = unit_rows(shared_b)
        probs, totals, diagonal = bucket_probs(unit_b, valid)
        grad_f = grad_b.astype(jnp.float32)
        grad_probs = jnp.einsum('bie,bje->bij', grad_f, value_b.astype(jnp.float32))
        grad_scores = jnp.where(diagonal[None], 0.0, probs * (grad_probs + offset_b[..., None]))
        scores_b = grad_scores.astype(jnp.bfloat16).astype(jnp.float32)
        unit_f = unit_b.astype(jnp.float32)
        grad_unit = sharpness * (jnp.einsum('bij,bje->bie', scores_b, unit_f) + jnp.einsum('bji,bje->bie', scores_b, unit_f))
        grad_in = (grad_unit - unit * lax.optimization_barrier(jnp.sum(unit * grad_unit, axis=-1, keepdims=True))) / length
        grad_val = jnp.einsum('bij,bie->bje', probs.astype(jnp.bfloat16).astype(jnp.float32), grad_f)
        grad_shared = grad_shared + to_tokens(grad_in.astype(jnp.bfloat16), flat).astype(jnp.float32)
        grad_values = grad_values + to_tokens(grad_val.astype(jnp.bfloat16), flat).astype(jnp.float32)
    return (attention, grad_shared.astype(jnp.bfloat16), grad_values.astype(jnp.bfloat16))

def reference(tokens, key_weight, value_weight, buckets, cotangent):
    shared = jnp.dot(tokens, key_weight, preferred_element_type=jnp.float32).astype(jnp.bfloat16)
    values = jnp.dot(tokens, value_weight, preferred_element_type=jnp.float32).astype(jnp.bfloat16)
    shared_heads = shared.reshape(TOKENS, HEADS, HEAD_SIZE).transpose(1, 0, 2)
    value_heads = values.reshape(TOKENS, HEADS, HEAD_SIZE).transpose(1, 0, 2)
    cot_heads = cotangent.reshape(TOKENS, HEADS, HEAD_SIZE).transpose(1, 0, 2)
    id_heads = buckets[..., 0].transpose(1, 0, 2).astype(jnp.int32)
    attention, grad_shared, grad_values = lax.map(head_pass, (shared_heads, value_heads, id_heads, cot_heads))
    attention = attention.transpose(1, 0, 2).reshape(TOKENS, D)
    grad_shared = grad_shared.transpose(1, 0, 2).reshape(TOKENS, D)
    grad_values = grad_values.transpose(1, 0, 2).reshape(TOKENS, D)
    grad_input = jnp.dot(grad_shared, key_weight.T, preferred_element_type=jnp.float32) + jnp.dot(grad_values, value_weight.T, preferred_element_type=jnp.float32)
    return (attention, grad_input)
```

```python
import jax
import jax.numpy as jnp
from jax import lax
from jax.experimental import pallas as pl
from jax.experimental.pallas import tpu as pltpu

P = jax.sharding.PartitionSpec
MESH = pl.DeviceIdType.MESH
f32, bf16, i32 = jnp.float32, jnp.bfloat16, jnp.int32

SHARP = 16.0
EMPTY = 1024.0
PEERS = 32
ROUNDS = 4
GROUP = 4


def iota(shape, dim):
    return lax.broadcasted_iota(i32, shape, dim)


def low_lanes(shape):
    return iota(shape, 1) % 128 < 64


def swap(x):
    return pltpu.roll(x, 64, 1)


def mm(a, b):
    return lax.dot_general(a, b, (((1,), (0,)), ((), ())), preferred_element_type=f32)


def mm_t(a, b):
    return lax.dot_general(a, b, (((1,), (1,)), ((), ())), preferred_element_type=f32)


def split2(x):
    high = x.astype(bf16)
    return high, (x - high.astype(f32)).astype(bf16)


def rank_codes(ids):
    ids_f = ids.astype(f32)
    columns = jnp.concatenate([ids_f, jnp.zeros((120, 128), f32)], axis=0).T
    before = iota((128, 128), 0) < iota((128, 128), 1)
    code = jnp.zeros((8, 128), f32)
    for r in range(ROUNDS):
        same = (columns[:, r : r + 1] == ids_f[r : r + 1, :]) & before
        rank = jnp.sum(jnp.where(same, 1.0, 0.0), axis=0, keepdims=True)
        code = jnp.where(iota((8, 128), 0) == r, ids_f[r : r + 1, :] + 128.0 * rank, code)
    return code.astype(i32)


def places(codes):
    bucket, rank = codes & 127, codes >> 7
    block = iota((8, 512), 1) >> 7
    slot = bucket * 4 + block
    both = jnp.concatenate([slot[:4].astype(f32), rank[:4].astype(f32)], axis=0)
    columns = []
    for m in range(GROUP):
        tile = both[:, 128 * m : 128 * m + 128]
        columns.append(jnp.concatenate([tile, jnp.zeros((120, 128), f32)], axis=0).T)
    return bucket, rank, slot, jnp.concatenate(columns, axis=0)


def slot_onehot(slot_row):
    return jnp.where(iota((512, 512), 0) == slot_row, 1.0, 0.0).astype(bf16)


def token_onehot(slot_column):
    return jnp.where(iota((512, 512), 1).astype(f32) == slot_column, 1.0, 0.0).astype(bf16)


def half_mask(rank_column):
    half = (iota((512, 128), 1) >> 6).astype(f32)
    return jnp.where(half == rank_column, 1.0, 0.0).astype(bf16)


def twice(pair):
    pair = pair.astype(f32)
    turned = swap(pair)
    low = low_lanes(pair.shape)
    return jnp.where(low, pair, turned).astype(bf16), jnp.where(low, turned, pair).astype(bf16)


def pack(onehot, rows, mask):
    right = jnp.concatenate([rows[0] * mask, rows[1] * mask, rows[2] * mask, mask], axis=1)
    out = mm(onehot, right)
    filled = out[:, 384:512] > 0.5
    return (
        out[:, 0:128].astype(bf16),
        out[:, 128:256].astype(bf16),
        jnp.where(filled, out[:, 256:384], EMPTY).astype(bf16),
    )


def regroup():
    p, c = iota((128, 128), 0), iota((128, 128), 1)
    hit = ((c >> 4) == ((p & 31) >> 2)) & (((c & 15) >> 2) == (p >> 5)) & ((c & 3) == (p & 3))
    return jnp.where(hit, 1.0, 0.0).astype(bf16)


def regroup_back():
    c, p = iota((128, 128), 0), iota((128, 128), 1)
    hit = ((c >> 4) == ((p & 31) >> 2)) & (((c & 15) >> 2) == (p >> 5)) & ((c & 3) == (p & 3))
    return jnp.where(hit, 1.0, 0.0).astype(bf16)


def half_ones():
    r, c = iota((256, 128), 0), iota((256, 128), 1)
    return jnp.where(((r & 127) >> 6) == (c >> 6), 1.0, 0.0).astype(bf16)


def half_sums(x, ones):
    high, low = split2(x)
    return mm(jnp.concatenate([high, low], axis=1), ones)


def on_rows(x):
    return jnp.concatenate([x, swap(x)], axis=0)


def on_rows_low(x):
    low = low_lanes(x.shape)
    return jnp.concatenate([jnp.where(low, x, 0.0), jnp.where(low, swap(x), 0.0)], axis=0)


def on_diagonal(x):
    low, turned = low_lanes(x.shape), swap(x)
    return jnp.concatenate(
        [jnp.where(low, x, 0.0), jnp.where(low, turned, 0.0), jnp.where(low, 0.0, turned), jnp.where(low, 0.0, x)],
        axis=0,
    ).astype(bf16)


def side_by_side(x):
    return jnp.concatenate([x[:128], x[128:]], axis=1)


def diagonal():
    return iota((256, 256), 0) == iota((256, 256), 1)


def owner_forward(shared, values, cot, ones):
    shared, values, cot = shared.astype(f32), values.astype(f32), cot.astype(f32)
    scale = lax.rsqrt(half_sums(shared * shared, ones) + 1e-6)
    unit = shared * scale
    scores = mm_t(on_rows_low(unit).astype(bf16), on_rows(unit).astype(bf16))
    weights = jnp.where(diagonal(), 1.0, jnp.exp(SHARP * scores))
    low = low_lanes((128, 128))
    valid = jnp.where(cot < 0.5 * EMPTY, 1.0, 0.0)
    turned = swap(valid)
    valid = jnp.concatenate([jnp.where(low, valid, turned), jnp.where(low, turned, valid)], axis=0)
    valid = jnp.concatenate([valid, valid], axis=1)
    totals = jnp.sum(weights * valid, axis=0, keepdims=True)
    along = mm_t(on_rows_low(values).astype(bf16), on_rows(cot).astype(bf16))
    products = jnp.sum(weights * along, axis=0, keepdims=True)
    numerator = mm(side_by_side(weights.astype(bf16)), on_diagonal(values))
    return weights, unit, scale, numerator.astype(bf16), totals, products


def owner_backward(weights, unit, scale, values, cot, rows, columns, ones):
    values, cot = values.astype(f32), cot.astype(f32)
    inv_row, along_row = rows
    wide = [jnp.broadcast_to(c, (128, 128)) for c in columns]
    inv_col = jnp.concatenate([wide[0], wide[1]], axis=0)
    along_col = jnp.concatenate([wide[2], wide[3]], axis=0)
    inv_col = jnp.concatenate([inv_col, inv_col], axis=1)
    along_col = jnp.concatenate([along_col, along_col], axis=1)
    value_rows, cot_rows = on_rows_low(values).astype(bf16), on_rows(cot).astype(bf16)
    right_left = mm_t(value_rows, cot_rows)
    left_right = mm_t(cot_rows, value_rows)
    inner = inv_row * (right_left - along_row) + inv_col * (left_right - along_col)
    grad = jnp.where(diagonal(), 0.0, weights * inner).astype(bf16)
    grad_unit = SHARP * mm(side_by_side(grad), on_diagonal(unit))
    low = low_lanes((128, 128))
    grad_round = jnp.where(low, wide[0], wide[1]) * cot
    grad_values = mm(side_by_side(weights.astype(bf16)), on_diagonal(grad_round))
    grad_shared = (grad_unit - unit * half_sums(unit * grad_unit, ones)) * scale
    return grad_shared.astype(bf16), grad_values.astype(bf16)


def square(x):
    return jnp.concatenate([x, jnp.zeros((128 - x.shape[0], 128), f32)], axis=0)


def place_onehot(bucket_row, block_row):
    return jnp.where(iota((128, 512), 0) == (bucket_row >> 2) * 4 + block_row, 1.0, 0.0).astype(bf16)


def token_scalars(turned, bucket, rank):
    block = iota((1, 512), 1) >> 7
    total, product = jnp.zeros((1, 512), f32), jnp.zeros((1, 512), f32)
    for r in range(ROUNDS):
        onehot = place_onehot(bucket[r : r + 1], block)
        high, low = split2(turned[16 * r : 16 * r + 16])
        picked = mm(jnp.concatenate([high, low], axis=1), jnp.concatenate([onehot, onehot], axis=0))
        hit = iota((8, 512), 0) == rank[r : r + 1] * 4 + (bucket[r : r + 1] & 3)
        total = total + jnp.sum(jnp.where(hit, picked[0:8], 0.0), axis=0, keepdims=True)
        product = product + jnp.sum(jnp.where(hit, picked[8:16], 0.0), axis=0, keepdims=True)
    inverse = 1.0 / total
    return inverse, product * inverse


def spread_scalars(inverse, along, bucket, rank):
    block = iota((1, 512), 1) >> 7
    out = []
    for r in range(ROUNDS):
        onehot = place_onehot(bucket[r : r + 1], block)
        hit = iota((8, 512), 0) == rank[r : r + 1] * 4 + (bucket[r : r + 1] & 3)
        left = jnp.concatenate([jnp.where(hit, inverse, 0.0), jnp.where(hit, along, 0.0)], axis=0)
        high, low = split2(left)
        both = mm_t(jnp.concatenate([high, low], axis=0), onehot)
        out.append(both[0:16] + both[16:32])
    return square(jnp.concatenate(out, axis=0))


def kernel(
    tok, kw, vw, ids, cot, att_out, gin_out,
    gat, wcat, sv_send, cot_send, code_send, sv_land, cot_land, code_land,
    onehot, onehot_t, masks, rows_x, slots_out, slots_in, tasks,
    w_keep, unit_keep, scale_keep, num_task, num_out, num_in, grad_task, grad_out, grad_in,
    z_rows, z_turn, z_out, z_in, q_turn, q_cols, q_out, q_in, acc,
    back_send, back_land, atth_send, atth_land, rs_send, rs_land,
    s0, r0, s1, r1, s2, r2, sn, rn, sg, rg, s3, r3, s4, r4, s6, r6, s7, r7,
):
    seq, y = lax.axis_index("seq"), lax.axis_index("head")
    z, xc = lax.div(seq, 8), lax.rem(seq, 8)
    zq, zr = lax.div(z, 4), lax.rem(z, 4)
    me = xc * 4 + y

    def slab(d):
        return (z * 8 + lax.div(d, 4), lax.rem(d, 4))

    def partner(i):
        return ((4 * i + y) * 8 + xc, zr)

    def arrived(ref, sem):
        pltpu.make_async_copy(ref, ref, sem).wait()

    def to_partner(i, src, land, send_sem, recv_sem):
        @pl.when(4 * i + y == z)
        def _():
            pltpu.make_async_copy(src, land.at[zq], recv_sem.at[zq]).start()

        @pl.when(4 * i + y != z)
        def _():
            pltpu.make_async_remote_copy(
                src, land.at[zq], send_sem.at[i], recv_sem.at[zq], device_id=partner(i), device_id_type=MESH
            ).start()

    def partner_sent(i, src, send_sem):
        @pl.when(4 * i + y != z)
        def _():
            arrived(src, send_sem.at[i])

    def to_slab(out_at, in_at, send_sem, recv_sem):
        pltpu.make_async_copy(out_at(me), in_at(me), recv_sem).start()

        def send(o, carry):
            d = lax.rem(me + o, PEERS)
            pltpu.make_async_remote_copy(
                out_at(d), in_at(me), send_sem, recv_sem, device_id=slab(d), device_id_type=MESH
            ).start()
            return carry

        lax.fori_loop(1, PEERS, send, 0)

    barrier = pltpu.get_barrier_semaphore()

    def greet(o, carry):
        pl.semaphore_signal(barrier, 1, device_id=slab(lax.rem(me + o, PEERS)), device_id_type=MESH)
        return carry

    lax.fori_loop(1, PEERS, greet, 0)
    for i in range(GROUP):

        @pl.when(4 * i + y != z)
        def _(i=i):
            pl.semaphore_signal(barrier, 1, device_id=partner(i), device_id_type=MESH)

    for k in range(GROUP):
        code_send[k] = rank_codes(ids[k])
    low64 = low_lanes((64, 128))
    for k in range(0, GROUP, 2):
        tile = cot[:, 64 * k : 64 * k + 128].astype(f32)
        top, bottom = tile[:64], tile[64:]
        cot_send[k] = jnp.where(low64, top, swap(bottom)).astype(bf16)
        cot_send[k + 1] = jnp.where(low64, swap(top), bottom).astype(bf16)

    pl.semaphore_wait(barrier, jnp.where(zr == y, 34, 35))

    for o in range(1, 4):
        pltpu.make_async_remote_copy(
            tok, gat.at[y], s0.at[o - 1], r0.at[o - 1], device_id=(seq, lax.rem(y + o, 4)), device_id_type=MESH
        ).start()
    for k in range(GROUP):
        to_partner(k, code_send.at[k], code_land, s1.at[0], r1.at[0])
        to_partner(k, cot_send.at[k], cot_land, s1.at[1], r1.at[1])

    def weave(c, carry):
        at = pl.ds(pl.multiple_of(c * 128, 128), 128)
        low = low_lanes((128, 128))
        for k in range(0, GROUP, 2):
            key, value = kw[at, 64 * k : 64 * k + 128].astype(f32), vw[at, 64 * k : 64 * k + 128].astype(f32)
            wcat[at, 128 * k : 128 * k + 128] = jnp.where(low, key, swap(value)).astype(bf16)
            wcat[at, 128 * k + 128 : 128 * k + 256] = jnp.where(low, swap(key), value).astype(bf16)
        return carry

    lax.fori_loop(0, 8, weave, 0)

    project = mm(tok[...], wcat[pl.ds(pl.multiple_of(y * 256, 256), 256), :])
    for o in range(1, 4):
        source = lax.rem(y + 4 - o, 4)
        arrived(gat.at[source], r0.at[o - 1])
        project = project + mm(gat[source], wcat[pl.ds(pl.multiple_of(source * 256, 256), 256), :])
    for k in range(GROUP):
        sv_send[k] = project[:, 128 * k : 128 * k + 128].astype(bf16)
        to_partner(k, sv_send.at[k], sv_land, s1.at[2], r1.at[2])

    for m in range(GROUP):
        arrived(code_land.at[m], r1.at[0, m])
    codes = jnp.concatenate([code_land[m] for m in range(GROUP)], axis=1)
    bucket, rank, slot, columns = places(codes)
    for r in range(ROUNDS):
        onehot[r] = slot_onehot(slot[r : r + 1])
        masks[r] = half_mask(columns[:, 4 + r : 5 + r])
    for m in range(GROUP):
        arrived(cot_land.at[m], r1.at[1, m])
        piece = cot_land[m].astype(f32)
        turned = swap(piece)
        rows_x[2, 128 * m : 128 * m + 64, :] = jnp.where(low64, piece, turned).astype(bf16)
        rows_x[2, 128 * m + 64 : 128 * m + 128, :] = jnp.where(low64, turned, piece).astype(bf16)
    for m in range(GROUP):
        arrived(sv_land.at[m], r1.at[2, m])
        first, second = twice(sv_land[m])
        rows_x[0, 128 * m : 128 * m + 128, :] = first
        rows_x[1, 128 * m : 128 * m + 128, :] = second

    def send_round(r, carry):
        parts = pack(onehot[r], (rows_x[0], rows_x[1], rows_x[2]), masks[r])
        for a in range(3):
            slots_out[r, a] = parts[a]
        to_slab(
            lambda d: slots_out.at[r, :, pl.ds(pl.multiple_of(d * 16, 16), 16), :],
            lambda d: slots_in.at[r, :, pl.ds(pl.multiple_of(d * 16, 16), 16), :],
            s2.at[r],
            r2.at[r],
        )
        return carry

    lax.fori_loop(0, ROUNDS, send_round, 0)

    for r in range(ROUNDS):
        onehot_t[r] = token_onehot(columns[:, r : r + 1])

    ones = half_ones()
    sort, unsort = regroup(), regroup_back()
    z_rows[...] = jnp.zeros((128, 128), f32)

    def forward_round(r, carry):
        arrived(slots_in.at[r], r2.at[r])
        for g in range(4):
            at = slice(128 * g, 128 * g + 128)
            moved = mm(sort, jnp.concatenate([slots_in[r, a, at, :] for a in range(3)], axis=1)).astype(bf16)
            for b in range(GROUP):
                for a in range(3):
                    tasks[r * 4 + b, a, 32 * g : 32 * g + 32, :] = moved[32 * b : 32 * b + 32, 128 * a : 128 * a + 128]

        def one(b, inner):
            t = r * 4 + b
            weights, unit, scale, numerator, totals, products = owner_forward(tasks[t, 0], tasks[t, 1], tasks[t, 2], ones)
            w_keep[t] = weights
            unit_keep[t] = unit
            scale_keep[t] = scale
            num_task[b] = numerator
            line = r * 16 + b
            z_rows[pl.ds(line, 1), :] = totals[:, :128]
            z_rows[pl.ds(line + 4, 1), :] = totals[:, 128:]
            z_rows[pl.ds(line + 8, 1), :] = products[:, :128]
            z_rows[pl.ds(line + 12, 1), :] = products[:, 128:]
            return inner

        lax.fori_loop(0, GROUP, one, 0)
        for g in range(4):
            moved = jnp.concatenate([num_task[b, 32 * g : 32 * g + 32, :] for b in range(GROUP)], axis=0)
            num_out[r, 128 * g : 128 * g + 128, :] = mm(unsort, moved).astype(bf16)
        to_slab(
            lambda d: num_out.at[r, pl.ds(pl.multiple_of(d * 16, 16), 16), :],
            lambda d: num_in.at[r, pl.ds(pl.multiple_of(d * 16, 16), 16), :],
            sn.at[r],
            rn.at[r],
        )
        return carry

    lax.fori_loop(0, ROUNDS, forward_round, 0)

    z_turn[...] = z_rows[...].T
    for d in range(PEERS):
        z_out[d] = z_turn[4 * d : 4 * d + 4, :]
    to_slab(lambda d: z_out.at[d], lambda d: z_in.at[d], s3.at[0], r3.at[0])
    arrived(z_in, r3.at[0])
    for d in range(PEERS):
        q_turn[4 * d : 4 * d + 4, :] = z_in[d]
    inverse, along = token_scalars(q_turn[...].T, bucket, rank)
    z_turn[...] = spread_scalars(inverse, along, bucket, rank).T
    for d in range(PEERS):
        q_out[d] = z_turn[4 * d : 4 * d + 4, :]
    to_slab(lambda d: q_out.at[d], lambda d: q_in.at[d], s4.at[0], r4.at[0])

    acc[:, 0:128] = jnp.zeros((512, 128), f32)

    def gather_out(r, carry):
        arrived(num_in.at[r], rn.at[r])
        acc[:, 0:128] += mm(onehot_t[r], num_in[r]) * masks[r].astype(f32)
        return carry

    lax.fori_loop(0, ROUNDS, gather_out, 0)
    low = low_lanes((128, 128))
    for m in range(GROUP):
        part = acc[128 * m : 128 * m + 128, 0:128]
        inv_col = jnp.broadcast_to(inverse[:, 128 * m : 128 * m + 128], (128, 128)).T
        result = (part + swap(part)) * inv_col
        atth_send[m] = jnp.where(low64, result[:64], result[64:]).astype(bf16)
        to_partner(m, atth_send.at[m], atth_land, s6.at[0], r6.at[0])

    arrived(q_in, r4.at[0])
    for d in range(PEERS):
        q_cols[4 * d : 4 * d + 4, :] = q_in[d]
    q_turn[...] = q_cols[...].T

    def backward_round(r, carry):
        def one(b, inner):
            t = r * 4 + b
            line = r * 16 + b
            near = pltpu.roll(q_cols[...], lax.rem(128 - line, 128), 1)
            rows = [
                jnp.concatenate([q_turn[pl.ds(line + s, 1), :], q_turn[pl.ds(line + s + 4, 1), :]], axis=1)
                for s in (0, 8)
            ]
            cols = [near[:, c : c + 1] for c in (0, 4, 8, 12)]
            grad_shared, grad_values = owner_backward(
                w_keep[t], unit_keep[t], scale_keep[t], tasks[t, 1], tasks[t, 2], rows, cols, ones
            )
            grad_task[b, 0] = grad_shared
            grad_task[b, 1] = grad_values
            return inner

        lax.fori_loop(0, GROUP, one, 0)
        for g in range(4):
            moved = [
                jnp.concatenate([grad_task[b, a, 32 * g : 32 * g + 32, :] for b in range(GROUP)], axis=0) for a in range(2)
            ]
            back = mm(unsort, jnp.concatenate(moved, axis=1)).astype(bf16)
            for a in range(2):
                grad_out[r, a, 128 * g : 128 * g + 128, :] = back[:, 128 * a : 128 * a + 128]
        to_slab(
            lambda d: grad_out.at[r, :, pl.ds(pl.multiple_of(d * 16, 16), 16), :],
            lambda d: grad_in.at[r, :, pl.ds(pl.multiple_of(d * 16, 16), 16), :],
            sg.at[r],
            rg.at[r],
        )
        return carry

    lax.fori_loop(0, ROUNDS, backward_round, 0)

    for k in range(GROUP):
        arrived(atth_land.at[k], r6.at[0, k])
    for k in range(0, GROUP, 2):
        first, second = atth_land[k].astype(f32), atth_land[k + 1].astype(f32)
        att_out[0:64, 64 * k : 64 * k + 128] = jnp.where(low64, first, swap(second))
        att_out[64:128, 64 * k : 64 * k + 128] = jnp.where(low64, swap(first), second)

    acc[...] = jnp.zeros((512, 256), f32)

    def gather_grads(r, carry):
        arrived(grad_in.at[r], rg.at[r])
        got = mm(onehot_t[r], jnp.concatenate([grad_in[r, 0], grad_in[r, 1]], axis=1))
        mask = masks[r].astype(f32)
        acc[...] += got * jnp.concatenate([mask, mask], axis=1)
        return carry

    lax.fori_loop(0, ROUNDS, gather_grads, 0)
    for m in range(GROUP):
        part = acc[128 * m : 128 * m + 128, :]
        first, second = part[:, :128], part[:, 128:]
        back_send[m] = jnp.where(low, first + swap(first), second + swap(second)).astype(bf16)
        to_partner(m, back_send.at[m], back_land, s6.at[1], r6.at[1])
    for k in range(GROUP):
        arrived(back_land.at[k], r6.at[1, k])

    left = jnp.concatenate([back_land[k] for k in range(GROUP)], axis=1)
    for o in range(1, 4):
        d = lax.rem(y + o, 4)
        rs_send[o - 1] = mm_t(left, wcat[pl.ds(pl.multiple_of(d * 256, 256), 256), :]).astype(bf16)
        pltpu.make_async_remote_copy(
            rs_send.at[o - 1], rs_land.at[o - 1], s7.at[o - 1], r7.at[o - 1], device_id=(seq, d), device_id_type=MESH
        ).start()
    total = mm_t(left, wcat[pl.ds(pl.multiple_of(y * 256, 256), 256), :])
    for o in range(1, 4):
        arrived(rs_land.at[o - 1], r7.at[o - 1])
        total = total + rs_land[o - 1].astype(f32)
    gin_out[...] = total

    for o in range(3):
        arrived(tok, s0.at[o])
        arrived(rs_send.at[o], s7.at[o])
    for k in range(GROUP):
        partner_sent(k, code_send.at[k], s1.at[0])
        partner_sent(k, cot_send.at[k], s1.at[1])
        partner_sent(k, sv_send.at[k], s1.at[2])
        partner_sent(k, atth_send.at[k], s6.at[0])
        partner_sent(k, back_send.at[k], s6.at[1])
    rest = pl.ds(0, 16 * (PEERS - 1))
    for r in range(ROUNDS):
        arrived(slots_out.at[r, :, rest, :], s2.at[r])
        arrived(num_out.at[r, rest, :], sn.at[r])
        arrived(grad_out.at[r, :, rest, :], sg.at[r])
    arrived(z_out.at[pl.ds(0, PEERS - 1)], s3.at[0])
    arrived(q_out.at[pl.ds(0, PEERS - 1)], s4.at[0])


def shards(tokens, key_weight, value_weight, buckets, cotangent):
    ids = jnp.pad(buckets[..., 0].transpose(1, 0, 2), ((0, 0), (0, 4), (0, 0)))
    vmem = pl.BlockSpec(memory_space=pltpu.VMEM)
    v, dma = pltpu.VMEM, pltpu.SemaphoreType.DMA
    scratch = [
        v((4, 128, 256), bf16),
        v((1024, 512), bf16),
        v((4, 128, 128), bf16),
        v((4, 64, 128), bf16),
        v((4, 8, 128), i32),
        v((4, 128, 128), bf16),
        v((4, 64, 128), bf16),
        v((4, 8, 128), i32),
        v((4, 512, 512), bf16),
        v((4, 512, 512), bf16),
        v((4, 512, 128), bf16),
        v((3, 512, 128), bf16),
        v((4, 3, 512, 128), bf16),
        v((4, 3, 512, 128), bf16),
        v((16, 3, 128, 128), bf16),
        v((16, 256, 256), f32),
        v((16, 128, 128), f32),
        v((16, 128, 128), f32),
        v((4, 128, 128), bf16),
        v((4, 512, 128), bf16),
        v((4, 512, 128), bf16),
        v((4, 2, 128, 128), bf16),
        v((4, 2, 512, 128), bf16),
        v((4, 2, 512, 128), bf16),
        v((128, 128), f32),
        v((128, 128), f32),
        v((32, 4, 128), f32),
        v((32, 4, 128), f32),
        v((128, 128), f32),
        v((128, 128), f32),
        v((32, 4, 128), f32),
        v((32, 4, 128), f32),
        v((512, 256), f32),
        v((4, 128, 128), bf16),
        v((4, 128, 128), bf16),
        v((4, 64, 128), bf16),
        v((4, 64, 128), bf16),
        v((3, 128, 256), bf16),
        v((3, 128, 256), bf16),
        dma((3,)), dma((3,)),
        dma((3, 4)), dma((3, 4)),
        dma((4,)), dma((4,)),
        dma((4,)), dma((4,)),
        dma((4,)), dma((4,)),
        dma((1,)), dma((1,)),
        dma((1,)), dma((1,)),
        dma((2, 4)), dma((2, 4)),
        dma((3,)), dma((3,)),
    ]
    return pl.pallas_call(
        kernel,
        out_shape=(jax.ShapeDtypeStruct((128, 256), f32), jax.ShapeDtypeStruct((128, 256), f32)),
        in_specs=[vmem] * 5,
        out_specs=(vmem, vmem),
        scratch_shapes=scratch,
        compiler_params=pltpu.CompilerParams(
            collective_id=0, has_side_effects=True, vmem_limit_bytes=50 * 1024 * 1024
        ),
    )(tokens, key_weight, value_weight, ids, cotangent)


def solution(mesh):
    in_specs = (
        P("seq", "head"),
        P(None, "head"),
        P(None, "head"),
        P(None, "head", "seq", None),
        P("seq", "head"),
    )
    out_specs = (P("seq", "head"), P("seq", "head"))
    return jax.shard_map(shards, mesh=mesh, in_specs=in_specs, out_specs=out_specs, check_vma=False)
```

```python
import jax
import jax.numpy as jnp
from jax import lax
from jax.experimental import pallas as pl
from jax.experimental.pallas import tpu as pltpu

P = jax.sharding.PartitionSpec
MESH = pl.DeviceIdType.MESH
f32, bf16, i32 = jnp.float32, jnp.bfloat16, jnp.int32

SHARP = 16.0
EMPTY = 1024.0
PEERS = 32
ROUNDS = 4
GROUP = 4


def iota(shape, dim):
    return lax.broadcasted_iota(i32, shape, dim)


def low_lanes(shape):
    return iota(shape, 1) % 128 < 64


def swap(x):
    return pltpu.roll(x, 64, 1)


def mm(a, b):
    return lax.dot_general(a, b, (((1,), (0,)), ((), ())), preferred_element_type=f32)


def mm_t(a, b):
    return lax.dot_general(a, b, (((1,), (1,)), ((), ())), preferred_element_type=f32)


def split2(x):
    high = x.astype(bf16)
    return high, (x - high.astype(f32)).astype(bf16)


def rank_codes(ids):
    rows = jnp.concatenate([ids[r].astype(f32) for r in range(ROUNDS)], axis=0)
    columns = jnp.concatenate([rows, jnp.zeros((112, 128), f32)], axis=0).T
    before = iota((128, 128), 0) < iota((128, 128), 1)
    codes = []
    for k in range(GROUP):
        code = jnp.zeros((8, 128), f32)
        for r in range(ROUNDS):
            at = 4 * r + k
            same = (columns[:, at : at + 1] == rows[at : at + 1, :]) & before
            rank = jnp.sum(jnp.where(same, 1.0, 0.0), axis=0, keepdims=True)
            code = jnp.where(iota((8, 128), 0) == r, rows[at : at + 1, :] + 128.0 * rank, code)
        codes.append(code.astype(i32))
    return codes


def places(codes):
    bucket, rank = codes & 127, codes >> 7
    block = iota((8, 512), 1) >> 7
    slot = bucket * 4 + block
    both = jnp.concatenate([slot[:4].astype(f32), rank[:4].astype(f32)], axis=0)
    columns = []
    for m in range(GROUP):
        tile = both[:, 128 * m : 128 * m + 128]
        columns.append(jnp.concatenate([tile, jnp.zeros((120, 128), f32)], axis=0).T)
    return bucket, rank, slot, jnp.concatenate(columns, axis=0)


def slot_onehot(slot_row):
    return jnp.where(iota((512, 512), 0) == slot_row, 1.0, 0.0).astype(bf16)


def token_onehot(slot_column):
    return jnp.where(iota((512, 512), 1).astype(f32) == slot_column, 1.0, 0.0).astype(bf16)


def half_mask(rank_column):
    half = (iota((512, 128), 1) >> 6).astype(f32)
    return jnp.where(half == rank_column, 1.0, 0.0).astype(bf16)


def halves(tile):
    top, bottom = tile[:64], tile[64:]
    low = low_lanes((64, 128))
    return jnp.where(low, top, swap(bottom)).astype(bf16), jnp.where(low, swap(top), bottom).astype(bf16)


def pack_cot(onehot, rows, mask):
    out = mm(onehot, jnp.concatenate([rows * mask, mask], axis=1))
    return jnp.where(out[:, 128:256] > 0.5, out[:, 0:128], EMPTY).astype(bf16)


def pack(onehot, rows, mask):
    return mm(onehot, rows * mask).astype(bf16)


def regroup():
    p, c = iota((128, 128), 0), iota((128, 128), 1)
    hit = ((c >> 4) == ((p & 31) >> 2)) & (((c & 15) >> 2) == (p >> 5)) & ((c & 3) == (p & 3))
    return jnp.where(hit, 1.0, 0.0).astype(bf16)


def regroup_back():
    c, p = iota((128, 128), 0), iota((128, 128), 1)
    hit = ((c >> 4) == ((p & 31) >> 2)) & (((c & 15) >> 2) == (p >> 5)) & ((c & 3) == (p & 3))
    return jnp.where(hit, 1.0, 0.0).astype(bf16)


def half_ones():
    r, c = iota((256, 128), 0), iota((256, 128), 1)
    return jnp.where(((r & 127) >> 6) == (c >> 6), 1.0, 0.0).astype(bf16)


def half_sums(x, ones):
    high, low = split2(x)
    return mm(jnp.concatenate([high, low], axis=1), ones)


def on_rows(x):
    return jnp.concatenate([x, swap(x)], axis=0)


def on_rows_low(x):
    low = low_lanes(x.shape)
    return jnp.concatenate([jnp.where(low, x, 0.0), jnp.where(low, swap(x), 0.0)], axis=0)


def on_diagonal(x):
    low, turned = low_lanes(x.shape), swap(x)
    return jnp.concatenate(
        [jnp.where(low, x, 0.0), jnp.where(low, turned, 0.0), jnp.where(low, 0.0, turned), jnp.where(low, 0.0, x)],
        axis=0,
    ).astype(bf16)


def side_by_side(x):
    return jnp.concatenate([x[:128], x[128:]], axis=1)


def diagonal():
    return iota((256, 256), 0) == iota((256, 256), 1)


def owner_scores(shared, cot, ones):
    shared = shared.astype(f32)
    scale = lax.rsqrt(half_sums(shared * shared, ones) + 1e-6)
    unit = shared * scale
    scores = mm_t(on_rows_low(unit).astype(bf16), on_rows(unit).astype(bf16))
    weights = jnp.where(diagonal(), 1.0, jnp.exp(SHARP * scores))
    low = low_lanes((128, 128))
    valid = jnp.where(cot.astype(f32) < 0.5 * EMPTY, 1.0, 0.0)
    turned = swap(valid)
    valid = jnp.concatenate([jnp.where(low, valid, turned), jnp.where(low, turned, valid)], axis=0)
    totals = jnp.sum(weights * jnp.concatenate([valid, valid], axis=1), axis=0, keepdims=True)
    return weights, side_by_side(weights.astype(bf16)), unit, scale, totals


def owner_outputs(weights, beside, values, cot):
    values, cot = values.astype(f32), cot.astype(f32)
    along = mm_t(on_rows_low(values).astype(bf16), on_rows(cot).astype(bf16))
    products = jnp.sum(weights * along, axis=0, keepdims=True)
    return mm(beside, on_diagonal(values)).astype(bf16), products


def owner_values(beside, cot, columns):
    wide = [jnp.broadcast_to(c, (128, 128)) for c in columns]
    grad_round = jnp.where(low_lanes((128, 128)), wide[0], wide[1]) * cot.astype(f32)
    return mm(beside, on_diagonal(grad_round)).astype(bf16), grad_round.astype(bf16)


def owner_shared(weights, unit, scale, values, grad_round, row, columns, ones):
    low = low_lanes((128, 128))
    wide = jnp.concatenate([jnp.broadcast_to(c, (128, 128)) for c in columns], axis=0)
    values, grad_round = values.astype(f32), grad_round.astype(f32)
    values_turned, grad_turned = swap(values), swap(grad_round)
    left = jnp.concatenate([jnp.where(low, grad_round, values_turned), jnp.where(low, grad_turned, values)], axis=0)
    right = jnp.concatenate([jnp.where(low, values, grad_turned), jnp.where(low, values_turned, grad_round)], axis=0)
    inner = mm_t(left.astype(bf16), right.astype(bf16)) - row - jnp.concatenate([wide, wide], axis=1)
    grad = jnp.where(diagonal(), 0.0, weights * inner).astype(bf16)
    grad_unit = SHARP * mm(side_by_side(grad), on_diagonal(unit))
    return ((grad_unit - unit * half_sums(unit * grad_unit, ones)) * scale).astype(bf16)


def own_tile(first, second):
    first, second = first.astype(f32), second.astype(f32)
    low = low_lanes((64, 128))
    return jnp.concatenate([jnp.where(low, first, swap(second)), jnp.where(low, swap(first), second)], axis=0)


def square(x):
    return jnp.concatenate([x, jnp.zeros((128 - x.shape[0], 128), f32)], axis=0)


def place_onehot(bucket_row, block_row):
    return jnp.where(iota((128, 512), 0) == (bucket_row >> 2) * 4 + block_row, 1.0, 0.0).astype(bf16)


def token_scalars(turned, bucket, rank):
    block = iota((1, 512), 1) >> 7
    total, product = jnp.zeros((1, 512), f32), jnp.zeros((1, 512), f32)
    for r in range(ROUNDS):
        onehot = place_onehot(bucket[r : r + 1], block)
        high, low = split2(turned[16 * r : 16 * r + 16])
        picked = mm(jnp.concatenate([high, low], axis=1), jnp.concatenate([onehot, onehot], axis=0))
        hit = iota((8, 512), 0) == rank[r : r + 1] * 4 + (bucket[r : r + 1] & 3)
        total = total + jnp.sum(jnp.where(hit, picked[0:8], 0.0), axis=0, keepdims=True)
        product = product + jnp.sum(jnp.where(hit, picked[8:16], 0.0), axis=0, keepdims=True)
    inverse = 1.0 / total
    return inverse, product * inverse * inverse


def spread_scalars(inverse, along, bucket, rank):
    block = iota((1, 512), 1) >> 7
    out = []
    for r in range(ROUNDS):
        onehot = place_onehot(bucket[r : r + 1], block)
        hit = iota((8, 512), 0) == rank[r : r + 1] * 4 + (bucket[r : r + 1] & 3)
        left = jnp.concatenate([jnp.where(hit, inverse, 0.0), jnp.where(hit, along, 0.0)], axis=0)
        high, low = split2(left)
        both = mm_t(jnp.concatenate([high, low], axis=0), onehot)
        out.append(both[0:16] + both[16:32])
    return square(jnp.concatenate(out, axis=0))


def kernel(
    tok, key_hbm, value_hbm, ids_hbm, cot_hbm, att_out, gin_out,
    gat, kw, vw, ids, cot, row_send, code_send, row_land, code_land,
    onehot, onehot_t, masks, rows_x, slots_out, slots_in, tasks,
    w_keep, beside_keep, unit_keep, scale_keep, round_keep,
    num_task, num_out, num_in, grad_task, grad_out, grad_in,
    z_rows, z_turn, z_out, z_in, q_turn, q_cols, q_out, q_in, acc, part,
    back_send, back_land, rs_send, rs_land,
    ld, s0, r0, s1, r1, s2, r2, sn, rn, sg, rg, s3, r3, s4, r4, s6, r6, s7, r7,
):
    seq, y = lax.axis_index("seq"), lax.axis_index("head")
    z, xc = lax.div(seq, 8), lax.rem(seq, 8)
    zq, zr = lax.div(z, 4), lax.rem(z, 4)
    me = xc * 4 + y
    rows = [lax.rem(y + o, 4) for o in range(4)]

    loads = ((ids_hbm, ids), (cot_hbm, cot), (tok, gat.at[y]), (key_hbm, kw), (value_hbm, vw))
    for i, (src, dst) in enumerate(loads):
        pltpu.make_async_copy(src, dst, ld.at[i]).start()

    def loaded(i):
        pltpu.make_async_copy(loads[i][0], loads[i][1], ld.at[i]).wait()

    def slab(d):
        return (z * 8 + lax.div(d, 4), lax.rem(d, 4))

    def partner(i):
        return ((4 * i + y) * 8 + xc, zr)

    def arrived(ref, sem):
        pltpu.make_async_copy(ref, ref, sem).wait()

    def to_partner(i, src, land, send_sem, recv_sem):
        @pl.when(4 * i + y == z)
        def _():
            pltpu.make_async_copy(src, land.at[zq], recv_sem.at[zq]).start()

        @pl.when(4 * i + y != z)
        def _():
            pltpu.make_async_remote_copy(
                src, land.at[zq], send_sem.at[i], recv_sem.at[zq], device_id=partner(i), device_id_type=MESH
            ).start()

    def partner_sent(i, src, send_sem):
        @pl.when(4 * i + y != z)
        def _():
            arrived(src, send_sem.at[i])

    def to_slab(out_at, in_at, send_sem, recv_sem):
        pltpu.make_async_copy(out_at(me), in_at(me), recv_sem).start()

        def start(column, row):
            d = column * 4 + row
            pltpu.make_async_remote_copy(
                out_at(d), in_at(me), send_sem, recv_sem, device_id=(z * 8 + column, row), device_id_type=MESH
            ).start()

        def send(o, carry):
            column = lax.rem(xc + o, 8)
            for row in rows:
                start(column, row)
            return carry

        for row in rows[1:]:
            start(xc, row)
        lax.fori_loop(1, 8, send, 0)

    barrier = pltpu.get_barrier_semaphore()

    def greet(o, carry):
        pl.semaphore_signal(barrier, 1, device_id=slab(lax.rem(me + o, PEERS)), device_id_type=MESH)
        return carry

    lax.fori_loop(1, PEERS, greet, 0)
    for i in range(GROUP):

        @pl.when(4 * i + y != z)
        def _(i=i):
            pl.semaphore_signal(barrier, 1, device_id=partner(i), device_id_type=MESH)

    loaded(0)
    for k, code in enumerate(rank_codes([ids[r] for r in range(ROUNDS)])):
        code_send[k] = code
    loaded(1)
    low64 = low_lanes((64, 128))
    for k in range(0, GROUP, 2):
        row_send[2, k], row_send[2, k + 1] = halves(cot[:, 64 * k : 64 * k + 128].astype(f32))

    pl.semaphore_wait(barrier, jnp.where(zr == y, 34, 35))

    for k in range(GROUP):
        to_partner(k, code_send.at[k], code_land, s1.at[0], r1.at[0])
    for o in range(1, 4):
        pltpu.make_async_remote_copy(
            tok, gat.at[y], s0.at[o - 1], r0.at[o - 1], device_id=(seq, lax.rem(y + o, 4)), device_id_type=MESH
        ).start()
    for k in range(GROUP):
        to_partner(k, row_send.at[2, k], row_land.at[2], s1.at[3], r1.at[3])

    for m in range(GROUP):
        arrived(code_land.at[m], r1.at[0, m])
    codes = jnp.concatenate([code_land[m] for m in range(GROUP)], axis=1)
    bucket, rank, slot, columns = places(codes)
    for r in range(ROUNDS):
        onehot[r] = slot_onehot(slot[r : r + 1])
        masks[r] = half_mask(columns[:, 4 + r : 5 + r])

    def piece(d):
        return pl.ds(pl.multiple_of(d * 16, 16), 16)

    def spread(a):
        for m in range(GROUP):
            arrived(row_land.at[a, m], r1.at[a + 1, m])
            landed = row_land[a, m].astype(f32)
            turned = swap(landed)
            rows_x[a, 128 * m : 128 * m + 64, :] = jnp.where(low64, landed, turned).astype(bf16)
            rows_x[a, 128 * m + 64 : 128 * m + 128, :] = jnp.where(low64, turned, landed).astype(bf16)

    spread(2)

    def pack_cots(r, carry):
        slots_out[2, r] = pack_cot(onehot[r], rows_x[2], masks[r])
        return carry

    lax.fori_loop(0, ROUNDS, pack_cots, 0)
    to_slab(lambda d: slots_out.at[2, :, piece(d), :], lambda d: slots_in.at[2, :, piece(d), :], s2.at[3], r2.at[3])

    for i in (2, 3, 4):
        loaded(i)
    for a, weight in enumerate((kw, vw)):
        result = mm(gat[y], weight[pl.ds(pl.multiple_of(y * 256, 256), 256), :])
        for o in range(1, 4):
            source = lax.rem(y + 4 - o, 4)
            if a == 0:
                arrived(gat.at[source], r0.at[o - 1])
            result = result + mm(gat[source], weight[pl.ds(pl.multiple_of(source * 256, 256), 256), :])
        for k in range(0, GROUP, 2):
            row_send[a, k], row_send[a, k + 1] = halves(result[:, 64 * k : 64 * k + 128])
        for k in range(GROUP):
            to_partner(k, row_send.at[a, k], row_land.at[a], s1.at[a + 1], r1.at[a + 1])

    spread(0)

    def pack_shared(r, carry):
        slots_out[0, r] = pack(onehot[r], rows_x[0], masks[r])
        return carry

    lax.fori_loop(0, ROUNDS, pack_shared, 0)
    to_slab(lambda d: slots_out.at[0, :, piece(d), :], lambda d: slots_in.at[0, :, piece(d), :], s2.at[0], r2.at[0])
    spread(1)

    def pack_values(p, carry):
        for i in range(2):
            slots_out[1, 2 * p + i] = pack(onehot[2 * p + i], rows_x[1], masks[2 * p + i])
        two = pl.ds(2 * p, 2)
        to_slab(
            lambda d: slots_out.at[1, two, piece(d), :],
            lambda d: slots_in.at[1, two, piece(d), :],
            s2.at[p + 1],
            r2.at[p + 1],
        )
        return carry

    lax.fori_loop(0, 2, pack_values, 0)

    for r in range(ROUNDS):
        onehot_t[r] = token_onehot(columns[:, r : r + 1])

    ones = half_ones()
    sort, unsort = regroup(), regroup_back()
    z_rows[...] = jnp.zeros((128, 128), f32)

    def sort_rows(a, r):
        for g in range(4):
            moved = mm(sort, slots_in[a, r, 128 * g : 128 * g + 128, :]).astype(bf16)
            for b in range(GROUP):
                tasks[r * 4 + b, a, 32 * g : 32 * g + 32, :] = moved[32 * b : 32 * b + 32]

    def sort_cots(r, carry):
        sort_rows(2, r)
        return carry

    arrived(slots_in.at[2], r2.at[3])
    lax.fori_loop(0, ROUNDS, sort_cots, 0)

    def scores_round(r, carry):
        sort_rows(0, r)
        for b in range(GROUP):
            t = r * 4 + b
            weights, beside, unit, scale, totals = owner_scores(tasks[t, 0], tasks[t, 2], ones)
            w_keep[t] = weights
            beside_keep[t] = beside
            unit_keep[t] = unit
            scale_keep[t] = scale
            line = r * 16 + b
            z_rows[pl.ds(line, 1), :] = totals[:, :128]
            z_rows[pl.ds(line + 4, 1), :] = totals[:, 128:]
        return carry

    arrived(slots_in.at[0], r2.at[0])
    lax.fori_loop(0, ROUNDS, scores_round, 0)

    def outputs_round(r):
        sort_rows(1, r)
        for b in range(GROUP):
            t = r * 4 + b
            numerator, products = owner_outputs(w_keep[t], beside_keep[t], tasks[t, 1], tasks[t, 2])
            num_task[b] = numerator
            line = r * 16 + b
            z_rows[pl.ds(line + 8, 1), :] = products[:, :128]
            z_rows[pl.ds(line + 12, 1), :] = products[:, 128:]
        for g in range(4):
            moved = jnp.concatenate([num_task[b, 32 * g : 32 * g + 32, :] for b in range(GROUP)], axis=0)
            num_out[r, 128 * g : 128 * g + 128, :] = mm(unsort, moved).astype(bf16)

    def outputs_pair(p, carry):
        arrived(slots_in.at[1, pl.ds(2 * p, 2)], r2.at[p + 1])
        for i in range(2):
            outputs_round(2 * p + i)
        return carry

    lax.fori_loop(0, 2, outputs_pair, 0)

    def send_numerators(p):
        two = pl.ds(2 * p, 2)
        to_slab(lambda d: num_out.at[two, piece(d), :], lambda d: num_in.at[two, piece(d), :], sn.at[p], rn.at[p])

    z_turn[...] = z_rows[...].T
    for d in range(PEERS):
        z_out[d] = z_turn[4 * d : 4 * d + 4, :]
    to_slab(lambda d: z_out.at[d], lambda d: z_in.at[d], s3.at[0], r3.at[0])
    send_numerators(0)
    arrived(z_in, r3.at[0])
    for d in range(PEERS):
        q_turn[4 * d : 4 * d + 4, :] = z_in[d]
    inverse, along = token_scalars(q_turn[...].T, bucket, rank)
    z_turn[...] = spread_scalars(inverse, along, bucket, rank).T
    for d in range(PEERS):
        q_out[d] = z_turn[4 * d : 4 * d + 4, :]
    to_slab(lambda d: q_out.at[d], lambda d: q_in.at[d], s4.at[0], r4.at[0])
    send_numerators(1)

    arrived(q_in, r4.at[0])
    for d in range(PEERS):
        q_cols[4 * d : 4 * d + 4, :] = q_in[d]
    q_turn[...] = q_cols[...].T

    def nearby(line):
        return pltpu.roll(q_cols[...], lax.rem(128 - line, 128), 1)

    def unsort_grads(a, r):
        for g in range(4):
            moved = jnp.concatenate([grad_task[b, 32 * g : 32 * g + 32, :] for b in range(GROUP)], axis=0)
            grad_out[a, r, 128 * g : 128 * g + 128, :] = mm(unsort, moved).astype(bf16)

    def values_pair(p, carry):
        for i in range(2):
            r = 2 * p + i
            for b in range(GROUP):
                t = r * 4 + b
                near = nearby(r * 16 + b)
                grad_values, grad_round = owner_values(beside_keep[t], tasks[t, 2], [near[:, c : c + 1] for c in (0, 4)])
                round_keep[t] = grad_round
                grad_task[b] = grad_values
            unsort_grads(0, r)
        two = pl.ds(2 * p, 2)
        to_slab(
            lambda d: grad_out.at[0, two, piece(d), :], lambda d: grad_in.at[0, two, piece(d), :], sg.at[p], rg.at[p]
        )
        return carry

    lax.fori_loop(0, 2, values_pair, 0)

    def shared_round(r, carry):
        for b in range(GROUP):
            t = r * 4 + b
            line = r * 16 + b
            near = nearby(line)
            row = jnp.concatenate([q_turn[pl.ds(line + 8, 1), :], q_turn[pl.ds(line + 12, 1), :]], axis=1)
            grad_task[b] = owner_shared(
                w_keep[t], unit_keep[t], scale_keep[t], tasks[t, 1], round_keep[t], row,
                [near[:, c : c + 1] for c in (8, 12)], ones,
            )
        unsort_grads(1, r)
        to_slab(
            lambda d: grad_out.at[1, r, piece(d), :], lambda d: grad_in.at[1, r, piece(d), :], sg.at[r + 2], rg.at[r + 2]
        )
        return carry

    lax.fori_loop(0, ROUNDS, shared_round, 0)

    def add(source, r):
        acc[...] += mm(onehot_t[r], source[r]) * masks[r].astype(f32)

    def summed(source, sems):
        acc[...] = jnp.zeros((512, 128), f32)

        def pair(p, carry):
            arrived(source.at[pl.ds(2 * p, 2)], sems.at[p])
            for i in range(2):
                add(source, 2 * p + i)
            return carry

        lax.fori_loop(0, 2, pair, 0)

    def send_back(a, scale):
        for m in range(GROUP):
            rows = acc[128 * m : 128 * m + 128, :]
            rows = rows + swap(rows)
            if scale is not None:
                rows = rows * jnp.broadcast_to(scale[:, 128 * m : 128 * m + 128], (128, 128)).T
            back_send[a, m] = jnp.where(low64, rows[:64], rows[64:]).astype(bf16)
            to_partner(m, back_send.at[a, m], back_land.at[a], s6.at[a], r6.at[a])

    def own_rows(a):
        for k in range(GROUP):
            arrived(back_land.at[a, k], r6.at[a, k])
        return [own_tile(back_land[a, k], back_land[a, k + 1]) for k in range(0, GROUP, 2)]

    summed(num_in, rn)
    send_back(0, inverse)
    summed(grad_in.at[0], rg)
    send_back(1, None)
    for k, tile in enumerate(own_rows(0)):
        att_out[:, 128 * k : 128 * k + 128] = tile
    acc[...] = jnp.zeros((512, 128), f32)

    def add_shared(r, carry):
        arrived(grad_in.at[1, r], rg.at[r + 2])
        add(grad_in.at[1], r)
        return carry

    lax.fori_loop(0, ROUNDS, add_shared, 0)
    send_back(2, None)

    left = jnp.concatenate(own_rows(1), axis=1).astype(bf16)
    for o in range(4):
        part[o] = mm_t(left, vw[pl.ds(pl.multiple_of(lax.rem(y + o, 4) * 256, 256), 256), :])
    left = jnp.concatenate(own_rows(2), axis=1).astype(bf16)
    for o in range(1, 4):
        d = lax.rem(y + o, 4)
        rs_send[o - 1] = (part[o] + mm_t(left, kw[pl.ds(pl.multiple_of(d * 256, 256), 256), :])).astype(bf16)
        pltpu.make_async_remote_copy(
            rs_send.at[o - 1], rs_land.at[o - 1], s7.at[o - 1], r7.at[o - 1], device_id=(seq, d), device_id_type=MESH
        ).start()
    total = part[0] + mm_t(left, kw[pl.ds(pl.multiple_of(y * 256, 256), 256), :])
    for o in range(1, 4):
        arrived(rs_land.at[o - 1], r7.at[o - 1])
        total = total + rs_land[o - 1].astype(f32)
    gin_out[...] = total

    for o in range(3):
        arrived(gat.at[o], s0.at[o])
        arrived(rs_send.at[o], s7.at[o])
    for k in range(GROUP):
        partner_sent(k, code_send.at[k], s1.at[0])
        for a in range(3):
            partner_sent(k, row_send.at[a, k], s1.at[a + 1])
            partner_sent(k, back_send.at[a, k], s6.at[a])
    rest = pl.ds(0, 16 * (PEERS - 1))
    arrived(slots_out.at[0, :, rest, :], s2.at[0])
    arrived(slots_out.at[2, :, rest, :], s2.at[3])
    for p in range(2):
        two = pl.ds(2 * p, 2)
        arrived(slots_out.at[1, two, rest, :], s2.at[p + 1])
        arrived(num_out.at[two, rest, :], sn.at[p])
        arrived(grad_out.at[0, two, rest, :], sg.at[p])
    for r in range(ROUNDS):
        arrived(grad_out.at[1, r, rest, :], sg.at[r + 2])
    arrived(z_out.at[pl.ds(0, PEERS - 1)], s3.at[0])
    arrived(q_out.at[pl.ds(0, PEERS - 1)], s4.at[0])


def shards(tokens, key_weight, value_weight, buckets, cotangent):
    vmem, hbm = pl.BlockSpec(memory_space=pltpu.VMEM), pl.BlockSpec(memory_space=pl.ANY)
    v, dma = pltpu.VMEM, pltpu.SemaphoreType.DMA
    scratch = [
        v((4, 128, 256), bf16),
        v((1024, 256), bf16),
        v((1024, 256), bf16),
        v((4, 4, 128), i32),
        v((128, 256), bf16),
        v((3, 4, 64, 128), bf16),
        v((4, 8, 128), i32),
        v((3, 4, 64, 128), bf16),
        v((4, 8, 128), i32),
        v((4, 512, 512), bf16),
        v((4, 512, 512), bf16),
        v((4, 512, 128), bf16),
        v((3, 512, 128), bf16),
        v((3, 4, 512, 128), bf16),
        v((3, 4, 512, 128), bf16),
        v((16, 3, 128, 128), bf16),
        v((16, 256, 256), f32),
        v((16, 128, 512), bf16),
        v((16, 128, 128), f32),
        v((16, 128, 128), f32),
        v((16, 128, 128), bf16),
        v((4, 128, 128), bf16),
        v((4, 512, 128), bf16),
        v((4, 512, 128), bf16),
        v((4, 128, 128), bf16),
        v((2, 4, 512, 128), bf16),
        v((2, 4, 512, 128), bf16),
        v((128, 128), f32),
        v((128, 128), f32),
        v((32, 4, 128), f32),
        v((32, 4, 128), f32),
        v((128, 128), f32),
        v((128, 128), f32),
        v((32, 4, 128), f32),
        v((32, 4, 128), f32),
        v((512, 128), f32),
        v((4, 128, 256), f32),
        v((3, 4, 64, 128), bf16),
        v((3, 4, 64, 128), bf16),
        v((3, 128, 256), bf16),
        v((3, 128, 256), bf16),
        dma((5,)),
        dma((3,)), dma((3,)),
        dma((4, 4)), dma((4, 4)),
        dma((4,)), dma((4,)),
        dma((2,)), dma((2,)),
        dma((6,)), dma((6,)),
        dma((1,)), dma((1,)),
        dma((1,)), dma((1,)),
        dma((3, 4)), dma((3, 4)),
        dma((3,)), dma((3,)),
    ]
    return pl.pallas_call(
        kernel,
        out_shape=(jax.ShapeDtypeStruct((128, 256), f32), jax.ShapeDtypeStruct((128, 256), f32)),
        in_specs=[hbm] * 5,
        out_specs=(vmem, vmem),
        scratch_shapes=scratch,
        compiler_params=pltpu.CompilerParams(
            collective_id=0, has_side_effects=True, vmem_limit_bytes=60 * 1024 * 1024
        ),
    )(tokens, key_weight, value_weight, buckets[..., 0], cotangent)


def solution(mesh):
    in_specs = (
        P("seq", "head"),
        P(None, "head"),
        P(None, "head"),
        P(None, "head", "seq", None),
        P("seq", "head"),
    )
    out_specs = (P("seq", "head"), P("seq", "head"))
    return jax.shard_map(shards, mesh=mesh, in_specs=in_specs, out_specs=out_specs, check_vma=False)
```

```python
import jax
import jax.numpy as jnp
from jax import lax
from jax.experimental import pallas as pl
from jax.experimental.pallas import tpu as pltpu

P = jax.sharding.PartitionSpec
MESH = pl.DeviceIdType.MESH
f32, bf16, i32 = jnp.float32, jnp.bfloat16, jnp.int32

SHARP = 16.0
EMPTY = 1024.0
PEERS = 32
ROUNDS = 4
GROUP = 4


def iota(shape, dim):
    return lax.broadcasted_iota(i32, shape, dim)


def low_lanes(shape):
    return iota(shape, 1) % 128 < 64


def swap(x):
    return pltpu.roll(x, 64, 1)


def mm(a, b):
    return lax.dot_general(a, b, (((1,), (0,)), ((), ())), preferred_element_type=f32)


def mm_t(a, b):
    return lax.dot_general(a, b, (((1,), (1,)), ((), ())), preferred_element_type=f32)


def split2(x):
    high = x.astype(bf16)
    return high, (x - high.astype(f32)).astype(bf16)


def rank_codes(ids):
    rows = jnp.concatenate([ids[r].astype(f32) for r in range(ROUNDS)], axis=0)
    columns = jnp.concatenate([rows, jnp.zeros((112, 128), f32)], axis=0).T
    before = iota((128, 128), 0) < iota((128, 128), 1)
    codes = []
    for k in range(GROUP):
        code = jnp.zeros((8, 128), f32)
        for r in range(ROUNDS):
            at = 4 * r + k
            same = (columns[:, at : at + 1] == rows[at : at + 1, :]) & before
            rank = jnp.sum(jnp.where(same, 1.0, 0.0), axis=0, keepdims=True)
            code = jnp.where(iota((8, 128), 0) == r, rows[at : at + 1, :] + 128.0 * rank, code)
        codes.append(code.astype(i32))
    return codes


def places(codes):
    bucket, rank = codes & 127, codes >> 7
    block = iota((8, 512), 1) >> 7
    slot = bucket * 4 + block
    both = jnp.concatenate([slot[:4].astype(f32), rank[:4].astype(f32)], axis=0)
    columns = []
    for m in range(GROUP):
        tile = both[:, 128 * m : 128 * m + 128]
        columns.append(jnp.concatenate([tile, jnp.zeros((120, 128), f32)], axis=0).T)
    return bucket, rank, slot, jnp.concatenate(columns, axis=0)


def slot_onehot(slot_row):
    return jnp.where(iota((512, 512), 0) == slot_row, 1.0, 0.0).astype(bf16)


def token_onehot(slot_column):
    return jnp.where(iota((512, 512), 1).astype(f32) == slot_column, 1.0, 0.0).astype(bf16)


def half_mask(rank_column):
    half = (iota((512, 128), 1) >> 6).astype(f32)
    return jnp.where(half == rank_column, 1.0, 0.0).astype(bf16)


def halves(tile):
    top, bottom = tile[:64], tile[64:]
    low = low_lanes((64, 128))
    return jnp.where(low, top, swap(bottom)).astype(bf16), jnp.where(low, swap(top), bottom).astype(bf16)


def pack_cot(onehot, rows, mask):
    out = mm(onehot, jnp.concatenate([rows * mask, mask], axis=1))
    return jnp.where(out[:, 128:256] > 0.5, out[:, 0:128], EMPTY).astype(bf16)


def pack(onehot, rows, mask):
    return mm(onehot, rows * mask).astype(bf16)


def regroup():
    p, c = iota((128, 128), 0), iota((128, 128), 1)
    hit = ((c >> 4) == ((p & 31) >> 2)) & (((c & 15) >> 2) == (p >> 5)) & ((c & 3) == (p & 3))
    return jnp.where(hit, 1.0, 0.0).astype(bf16)


def regroup_back():
    c, p = iota((128, 128), 0), iota((128, 128), 1)
    hit = ((c >> 4) == ((p & 31) >> 2)) & (((c & 15) >> 2) == (p >> 5)) & ((c & 3) == (p & 3))
    return jnp.where(hit, 1.0, 0.0).astype(bf16)


def half_ones():
    r, c = iota((256, 128), 0), iota((256, 128), 1)
    return jnp.where(((r & 127) >> 6) == (c >> 6), 1.0, 0.0).astype(bf16)


def half_sums(x, ones):
    high, low = split2(x)
    return mm(jnp.concatenate([high, low], axis=1), ones)


def on_rows(x):
    return jnp.concatenate([x, swap(x)], axis=0)


def on_rows_low(x):
    low = low_lanes(x.shape)
    return jnp.concatenate([jnp.where(low, x, 0.0), jnp.where(low, swap(x), 0.0)], axis=0)


def on_diagonal(x):
    low, turned = low_lanes(x.shape), swap(x)
    return jnp.concatenate(
        [jnp.where(low, x, 0.0), jnp.where(low, turned, 0.0), jnp.where(low, 0.0, turned), jnp.where(low, 0.0, x)],
        axis=0,
    ).astype(bf16)


def side_by_side(x):
    return jnp.concatenate([x[:128], x[128:]], axis=1)


def diagonal():
    return iota((256, 256), 0) == iota((256, 256), 1)


def owner_scores(shared, cot, ones):
    shared = shared.astype(f32)
    scale = lax.rsqrt(half_sums(shared * shared, ones) + 1e-6)
    unit = shared * scale
    scores = mm_t(on_rows_low(unit).astype(bf16), on_rows(unit).astype(bf16))
    weights = jnp.where(diagonal(), 1.0, jnp.exp(SHARP * scores))
    low = low_lanes((128, 128))
    valid = jnp.where(cot.astype(f32) < 0.5 * EMPTY, 1.0, 0.0)
    turned = swap(valid)
    valid = jnp.concatenate([jnp.where(low, valid, turned), jnp.where(low, turned, valid)], axis=0)
    totals = jnp.sum(weights * jnp.concatenate([valid, valid], axis=1), axis=0, keepdims=True)
    return weights, side_by_side(weights.astype(bf16)), unit, scale, totals


def owner_outputs(weights, beside, values, cot):
    values, cot = values.astype(f32), cot.astype(f32)
    along = mm_t(on_rows_low(values).astype(bf16), on_rows(cot).astype(bf16))
    products = jnp.sum(weights * along, axis=0, keepdims=True)
    return mm(beside, on_diagonal(values)).astype(bf16), products


def owner_values(beside, cot, columns):
    wide = [jnp.broadcast_to(c, (128, 128)) for c in columns]
    grad_round = jnp.where(low_lanes((128, 128)), wide[0], wide[1]) * cot.astype(f32)
    return mm(beside, on_diagonal(grad_round)).astype(bf16), grad_round.astype(bf16)


def owner_shared(weights, unit, scale, values, grad_round, row, columns, ones):
    low = low_lanes((128, 128))
    wide = jnp.concatenate([jnp.broadcast_to(c, (128, 128)) for c in columns], axis=0)
    values, grad_round = values.astype(f32), grad_round.astype(f32)
    values_turned, grad_turned = swap(values), swap(grad_round)
    left = jnp.concatenate([jnp.where(low, grad_round, values_turned), jnp.where(low, grad_turned, values)], axis=0)
    right = jnp.concatenate([jnp.where(low, values, grad_turned), jnp.where(low, values_turned, grad_round)], axis=0)
    inner = mm_t(left.astype(bf16), right.astype(bf16)) - row - jnp.concatenate([wide, wide], axis=1)
    grad = jnp.where(diagonal(), 0.0, weights * inner).astype(bf16)
    grad_unit = SHARP * mm(side_by_side(grad), on_diagonal(unit))
    return ((grad_unit - unit * half_sums(unit * grad_unit, ones)) * scale).astype(bf16)


def own_tile(first, second):
    first, second = first.astype(f32), second.astype(f32)
    low = low_lanes((64, 128))
    return jnp.concatenate([jnp.where(low, first, swap(second)), jnp.where(low, swap(first), second)], axis=0)


def square(x):
    return jnp.concatenate([x, jnp.zeros((128 - x.shape[0], 128), f32)], axis=0)


def place_onehot(bucket_row, block_row):
    return jnp.where(iota((128, 512), 0) == (bucket_row >> 2) * 4 + block_row, 1.0, 0.0).astype(bf16)


def token_scalars(turned, bucket, rank):
    block = iota((1, 512), 1) >> 7
    total, product = jnp.zeros((1, 512), f32), jnp.zeros((1, 512), f32)
    for r in range(ROUNDS):
        onehot = place_onehot(bucket[r : r + 1], block)
        high, low = split2(turned[16 * r : 16 * r + 16])
        picked = mm(jnp.concatenate([high, low], axis=1), jnp.concatenate([onehot, onehot], axis=0))
        hit = iota((8, 512), 0) == rank[r : r + 1] * 4 + (bucket[r : r + 1] & 3)
        total = total + jnp.sum(jnp.where(hit, picked[0:8], 0.0), axis=0, keepdims=True)
        product = product + jnp.sum(jnp.where(hit, picked[8:16], 0.0), axis=0, keepdims=True)
    inverse = 1.0 / total
    return inverse, product * inverse * inverse


def spread_scalars(inverse, along, bucket, rank):
    block = iota((1, 512), 1) >> 7
    out = []
    for r in range(ROUNDS):
        onehot = place_onehot(bucket[r : r + 1], block)
        hit = iota((8, 512), 0) == rank[r : r + 1] * 4 + (bucket[r : r + 1] & 3)
        left = jnp.concatenate([jnp.where(hit, inverse, 0.0), jnp.where(hit, along, 0.0)], axis=0)
        high, low = split2(left)
        both = mm_t(jnp.concatenate([high, low], axis=0), onehot)
        out.append(both[0:16] + both[16:32])
    return square(jnp.concatenate(out, axis=0))


def kernel(
    tok, key_hbm, value_hbm, ids_hbm, cot_hbm, att_out, gin_out,
    gat, kw, vw, ids, cot, row_send, code_send, row_land, code_land,
    onehot, onehot_t, masks, rows_x, slots_out, slots_in, tasks,
    w_keep, beside_keep, unit_keep, scale_keep, round_keep,
    num_task, num_out, num_in, grad_task, grad_out, grad_in,
    z_rows, z_turn, z_out, z_in, q_turn, q_cols, q_out, q_in, acc, part,
    back_send, back_land, rs_send, rs_land,
    ld, s0, r0, s1, r1, s2, r2, sn, rn, sg, rg, s3, r3, s4, r4, s6, r6, s7, r7,
):
    seq, y = lax.axis_index("seq"), lax.axis_index("head")
    z, xc = lax.div(seq, 8), lax.rem(seq, 8)
    zq, zr = lax.div(z, 4), lax.rem(z, 4)
    me = xc * 4 + y
    rows = [lax.rem(y + o, 4) for o in range(4)]

    loads = ((ids_hbm, ids), (cot_hbm, cot), (tok, gat.at[y]), (key_hbm, kw), (value_hbm, vw))
    for i, (src, dst) in enumerate(loads):
        pltpu.make_async_copy(src, dst, ld.at[i]).start()

    def loaded(i):
        pltpu.make_async_copy(loads[i][0], loads[i][1], ld.at[i]).wait()

    def slab(d):
        return (z * 8 + lax.div(d, 4), lax.rem(d, 4))

    first = z < 4
    turn = jnp.where(first, 0, lax.rem(z + 2, 3) + 1)
    block = jnp.where(first, z, lax.div(z + 2, 3) - 2)
    alone = first & (z == y)

    def head_place(i):
        return ((4 * i + y) * 8 + xc, lax.rem(turn + y, 4))

    def block_home(i):
        back = lax.rem(y + 4 - zr, 4)
        return (jnp.where(back == 0, i, 3 + 3 * i + back) * 8 + xc, zr)

    def arrived(ref, sem):
        pltpu.make_async_copy(ref, ref, sem).wait()

    to_head = (head_place, block, lambda i: alone & (zq == i))
    to_home = (block_home, zq, lambda i: alone & (zr == i))

    def to_partner(way, i, src, land, send_sem, recv_sem):
        partner, slot, itself = way

        @pl.when(itself(i))
        def _():
            pltpu.make_async_copy(src, land.at[slot], recv_sem.at[slot]).start()

        @pl.when(jnp.logical_not(itself(i)))
        def _():
            pltpu.make_async_remote_copy(
                src, land.at[slot], send_sem.at[i], recv_sem.at[slot], device_id=partner(i), device_id_type=MESH
            ).start()

    def partner_sent(way, i, src, send_sem):
        @pl.when(jnp.logical_not(way[2](i)))
        def _():
            arrived(src, send_sem.at[i])

    def to_slab(out_at, in_at, send_sem, recv_sem):
        pltpu.make_async_copy(out_at(me), in_at(me), recv_sem).start()

        def start(column, row):
            d = column * 4 + row
            pltpu.make_async_remote_copy(
                out_at(d), in_at(me), send_sem, recv_sem, device_id=(z * 8 + column, row), device_id_type=MESH
            ).start()

        def send(o, carry):
            column = lax.rem(xc + o, 8)
            for row in rows:
                start(column, row)
            return carry

        for row in rows[1:]:
            start(xc, row)
        lax.fori_loop(1, 8, send, 0)

    barrier = pltpu.get_barrier_semaphore()

    def greet(o, carry):
        pl.semaphore_signal(barrier, 1, device_id=slab(lax.rem(me + o, PEERS)), device_id_type=MESH)
        return carry

    lax.fori_loop(1, PEERS, greet, 0)
    for i in range(GROUP):

        for way in (to_head, to_home):

            @pl.when(jnp.logical_not(way[2](i)))
            def _(i=i, way=way):
                pl.semaphore_signal(barrier, 1, device_id=way[0](i), device_id_type=MESH)

    loaded(0)
    for k, code in enumerate(rank_codes([ids[r] for r in range(ROUNDS)])):
        code_send[k] = code
    loaded(1)
    low64 = low_lanes((64, 128))
    for k in range(0, GROUP, 2):
        row_send[2, k], row_send[2, k + 1] = halves(cot[:, 64 * k : 64 * k + 128].astype(f32))

    pl.semaphore_wait(barrier, jnp.where(alone, 37, 39))

    for k in range(GROUP):
        to_partner(to_head, k, code_send.at[k], code_land, s1.at[0], r1.at[0])
    for o in range(1, 4):
        pltpu.make_async_remote_copy(
            tok, gat.at[y], s0.at[o - 1], r0.at[o - 1], device_id=(seq, lax.rem(y + o, 4)), device_id_type=MESH
        ).start()
    for k in range(GROUP):
        to_partner(to_head, k, row_send.at[2, k], row_land.at[2], s1.at[3], r1.at[3])

    for m in range(GROUP):
        arrived(code_land.at[m], r1.at[0, m])
    codes = jnp.concatenate([code_land[m] for m in range(GROUP)], axis=1)
    bucket, rank, slot, columns = places(codes)
    for r in range(ROUNDS):
        onehot[r] = slot_onehot(slot[r : r + 1])
        masks[r] = half_mask(columns[:, 4 + r : 5 + r])

    def piece(d):
        return pl.ds(pl.multiple_of(d * 16, 16), 16)

    def spread(a):
        for m in range(GROUP):
            arrived(row_land.at[a, m], r1.at[a + 1, m])
            landed = row_land[a, m].astype(f32)
            turned = swap(landed)
            rows_x[a, 128 * m : 128 * m + 64, :] = jnp.where(low64, landed, turned).astype(bf16)
            rows_x[a, 128 * m + 64 : 128 * m + 128, :] = jnp.where(low64, turned, landed).astype(bf16)

    for i in (2, 3, 4):
        loaded(i)
    for a, weight in enumerate((kw, vw)):
        result = mm(gat[y], weight[pl.ds(pl.multiple_of(y * 256, 256), 256), :])
        for o in range(1, 4):
            source = lax.rem(y + 4 - o, 4)
            if a == 0:
                arrived(gat.at[source], r0.at[o - 1])
            result = result + mm(gat[source], weight[pl.ds(pl.multiple_of(source * 256, 256), 256), :])
        for k in range(0, GROUP, 2):
            row_send[a, k], row_send[a, k + 1] = halves(result[:, 64 * k : 64 * k + 128])
        for k in range(GROUP):
            to_partner(to_head, k, row_send.at[a, k], row_land.at[a], s1.at[a + 1], r1.at[a + 1])

    spread(2)

    def pack_cots(r, carry):
        slots_out[2, r] = pack_cot(onehot[r], rows_x[2], masks[r])
        return carry

    lax.fori_loop(0, ROUNDS, pack_cots, 0)
    to_slab(lambda d: slots_out.at[2, :, piece(d), :], lambda d: slots_in.at[2, :, piece(d), :], s2.at[3], r2.at[3])

    spread(0)

    def pack_shared(r, carry):
        slots_out[0, r] = pack(onehot[r], rows_x[0], masks[r])
        return carry

    lax.fori_loop(0, ROUNDS, pack_shared, 0)
    to_slab(lambda d: slots_out.at[0, :, piece(d), :], lambda d: slots_in.at[0, :, piece(d), :], s2.at[0], r2.at[0])
    spread(1)

    def pack_values(p, carry):
        for i in range(2):
            slots_out[1, 2 * p + i] = pack(onehot[2 * p + i], rows_x[1], masks[2 * p + i])
        two = pl.ds(2 * p, 2)
        to_slab(
            lambda d: slots_out.at[1, two, piece(d), :],
            lambda d: slots_in.at[1, two, piece(d), :],
            s2.at[p + 1],
            r2.at[p + 1],
        )
        return carry

    lax.fori_loop(0, 2, pack_values, 0)

    for r in range(ROUNDS):
        onehot_t[r] = token_onehot(columns[:, r : r + 1])

    ones = half_ones()
    sort, unsort = regroup(), regroup_back()
    z_rows[...] = jnp.zeros((128, 128), f32)

    def sort_rows(a, r):
        for g in range(4):
            moved = mm(sort, slots_in[a, r, 128 * g : 128 * g + 128, :]).astype(bf16)
            for b in range(GROUP):
                tasks[r * 4 + b, a, 32 * g : 32 * g + 32, :] = moved[32 * b : 32 * b + 32]

    def sort_cots(r, carry):
        sort_rows(2, r)
        return carry

    arrived(slots_in.at[2], r2.at[3])
    lax.fori_loop(0, ROUNDS, sort_cots, 0)

    def scores_round(r, carry):
        sort_rows(0, r)
        for b in range(GROUP):
            t = r * 4 + b
            weights, beside, unit, scale, totals = owner_scores(tasks[t, 0], tasks[t, 2], ones)
            w_keep[t] = weights
            beside_keep[t] = beside
            unit_keep[t] = unit
            scale_keep[t] = scale
            line = r * 16 + b
            z_rows[pl.ds(line, 1), :] = totals[:, :128]
            z_rows[pl.ds(line + 4, 1), :] = totals[:, 128:]
        return carry

    arrived(slots_in.at[0], r2.at[0])
    lax.fori_loop(0, ROUNDS, scores_round, 0)

    def outputs_round(r):
        sort_rows(1, r)
        for b in range(GROUP):
            t = r * 4 + b
            numerator, products = owner_outputs(w_keep[t], beside_keep[t], tasks[t, 1], tasks[t, 2])
            num_task[b] = numerator
            line = r * 16 + b
            z_rows[pl.ds(line + 8, 1), :] = products[:, :128]
            z_rows[pl.ds(line + 12, 1), :] = products[:, 128:]
        for g in range(4):
            moved = jnp.concatenate([num_task[b, 32 * g : 32 * g + 32, :] for b in range(GROUP)], axis=0)
            num_out[r, 128 * g : 128 * g + 128, :] = mm(unsort, moved).astype(bf16)

    def outputs_pair(p, carry):
        arrived(slots_in.at[1, pl.ds(2 * p, 2)], r2.at[p + 1])
        for i in range(2):
            outputs_round(2 * p + i)
        return carry

    lax.fori_loop(0, 2, outputs_pair, 0)

    def send_numerators(p):
        two = pl.ds(2 * p, 2)
        to_slab(lambda d: num_out.at[two, piece(d), :], lambda d: num_in.at[two, piece(d), :], sn.at[p], rn.at[p])

    z_turn[...] = z_rows[...].T
    for d in range(PEERS):
        z_out[d] = z_turn[4 * d : 4 * d + 4, :]
    to_slab(lambda d: z_out.at[d], lambda d: z_in.at[d], s3.at[0], r3.at[0])
    send_numerators(0)
    arrived(z_in, r3.at[0])
    for d in range(PEERS):
        q_turn[4 * d : 4 * d + 4, :] = z_in[d]
    inverse, along = token_scalars(q_turn[...].T, bucket, rank)
    z_turn[...] = spread_scalars(inverse, along, bucket, rank).T
    for d in range(PEERS):
        q_out[d] = z_turn[4 * d : 4 * d + 4, :]
    to_slab(lambda d: q_out.at[d], lambda d: q_in.at[d], s4.at[0], r4.at[0])
    send_numerators(1)

    def add(source, r):
        acc[...] += mm(onehot_t[r], source[r]) * masks[r].astype(f32)

    def summed(source, sems):
        acc[...] = jnp.zeros((512, 128), f32)

        def pair(p, carry):
            arrived(source.at[pl.ds(2 * p, 2)], sems.at[p])
            for i in range(2):
                add(source, 2 * p + i)
            return carry

        lax.fori_loop(0, 2, pair, 0)

    def send_back(a, scale):
        for m in range(GROUP):
            rows = acc[128 * m : 128 * m + 128, :]
            rows = rows + swap(rows)
            if scale is not None:
                rows = rows * jnp.broadcast_to(scale[:, 128 * m : 128 * m + 128], (128, 128)).T
            back_send[a, m] = jnp.where(low64, rows[:64], rows[64:]).astype(bf16)
            to_partner(to_home, m, back_send.at[a, m], back_land.at[a], s6.at[a], r6.at[a])

    def own_rows(a):
        for k in range(GROUP):
            arrived(back_land.at[a, k], r6.at[a, k])
        return [own_tile(back_land[a, k], back_land[a, k + 1]) for k in range(0, GROUP, 2)]

    arrived(q_in, r4.at[0])
    for d in range(PEERS):
        q_cols[4 * d : 4 * d + 4, :] = q_in[d]
    q_turn[...] = q_cols[...].T

    def nearby(line):
        return pltpu.roll(q_cols[...], lax.rem(128 - line, 128), 1)

    def unsort_grads(a, r):
        for g in range(4):
            moved = jnp.concatenate([grad_task[b, 32 * g : 32 * g + 32, :] for b in range(GROUP)], axis=0)
            grad_out[a, r, 128 * g : 128 * g + 128, :] = mm(unsort, moved).astype(bf16)

    def values_pair(p, carry):
        for i in range(2):
            r = 2 * p + i
            for b in range(GROUP):
                t = r * 4 + b
                near = nearby(r * 16 + b)
                grad_values, grad_round = owner_values(beside_keep[t], tasks[t, 2], [near[:, c : c + 1] for c in (0, 4)])
                round_keep[t] = grad_round
                grad_task[b] = grad_values
            unsort_grads(0, r)
        two = pl.ds(2 * p, 2)
        to_slab(
            lambda d: grad_out.at[0, two, piece(d), :], lambda d: grad_in.at[0, two, piece(d), :], sg.at[p], rg.at[p]
        )
        return carry

    lax.fori_loop(0, 2, values_pair, 0)
    summed(num_in, rn)
    send_back(0, inverse)

    def shared_round(r, carry):
        for b in range(GROUP):
            t = r * 4 + b
            line = r * 16 + b
            near = nearby(line)
            row = jnp.concatenate([q_turn[pl.ds(line + 8, 1), :], q_turn[pl.ds(line + 12, 1), :]], axis=1)
            grad_task[b] = owner_shared(
                w_keep[t], unit_keep[t], scale_keep[t], tasks[t, 1], round_keep[t], row,
                [near[:, c : c + 1] for c in (8, 12)], ones,
            )
        unsort_grads(1, r)
        to_slab(
            lambda d: grad_out.at[1, r, piece(d), :], lambda d: grad_in.at[1, r, piece(d), :], sg.at[r + 2], rg.at[r + 2]
        )
        return carry

    lax.fori_loop(0, ROUNDS, shared_round, 0)

    summed(grad_in.at[0], rg)
    send_back(1, None)
    acc[...] = jnp.zeros((512, 128), f32)

    def add_shared(r, carry):
        arrived(grad_in.at[1, r], rg.at[r + 2])
        add(grad_in.at[1], r)
        return carry

    lax.fori_loop(0, ROUNDS, add_shared, 0)
    send_back(2, None)
    for k, tile in enumerate(own_rows(0)):
        att_out[:, 128 * k : 128 * k + 128] = tile

    left = jnp.concatenate(own_rows(1), axis=1).astype(bf16)
    for o in range(4):
        part[o] = mm_t(left, vw[pl.ds(pl.multiple_of(lax.rem(y + o, 4) * 256, 256), 256), :])
    left = jnp.concatenate(own_rows(2), axis=1).astype(bf16)
    for o in range(1, 4):
        d = lax.rem(y + o, 4)
        rs_send[o - 1] = (part[o] + mm_t(left, kw[pl.ds(pl.multiple_of(d * 256, 256), 256), :])).astype(bf16)
        pltpu.make_async_remote_copy(
            rs_send.at[o - 1], rs_land.at[o - 1], s7.at[o - 1], r7.at[o - 1], device_id=(seq, d), device_id_type=MESH
        ).start()
    total = part[0] + mm_t(left, kw[pl.ds(pl.multiple_of(y * 256, 256), 256), :])
    for o in range(1, 4):
        arrived(rs_land.at[o - 1], r7.at[o - 1])
        total = total + rs_land[o - 1].astype(f32)
    gin_out[...] = total

    for o in range(3):
        arrived(gat.at[o], s0.at[o])
        arrived(rs_send.at[o], s7.at[o])
    for k in range(GROUP):
        partner_sent(to_head, k, code_send.at[k], s1.at[0])
        for a in range(3):
            partner_sent(to_head, k, row_send.at[a, k], s1.at[a + 1])
            partner_sent(to_home, k, back_send.at[a, k], s6.at[a])
    rest = pl.ds(0, 16 * (PEERS - 1))
    arrived(slots_out.at[0, :, rest, :], s2.at[0])
    arrived(slots_out.at[2, :, rest, :], s2.at[3])
    for p in range(2):
        two = pl.ds(2 * p, 2)
        arrived(slots_out.at[1, two, rest, :], s2.at[p + 1])
        arrived(num_out.at[two, rest, :], sn.at[p])
        arrived(grad_out.at[0, two, rest, :], sg.at[p])
    for r in range(ROUNDS):
        arrived(grad_out.at[1, r, rest, :], sg.at[r + 2])
    arrived(z_out.at[pl.ds(0, PEERS - 1)], s3.at[0])
    arrived(q_out.at[pl.ds(0, PEERS - 1)], s4.at[0])


def shards(tokens, key_weight, value_weight, buckets, cotangent):
    vmem, hbm = pl.BlockSpec(memory_space=pltpu.VMEM), pl.BlockSpec(memory_space=pl.ANY)
    v, dma = pltpu.VMEM, pltpu.SemaphoreType.DMA
    scratch = [
        v((4, 128, 256), bf16),
        v((1024, 256), bf16),
        v((1024, 256), bf16),
        v((4, 4, 128), i32),
        v((128, 256), bf16),
        v((3, 4, 64, 128), bf16),
        v((4, 8, 128), i32),
        v((3, 4, 64, 128), bf16),
        v((4, 8, 128), i32),
        v((4, 512, 512), bf16),
        v((4, 512, 512), bf16),
        v((4, 512, 128), bf16),
        v((3, 512, 128), bf16),
        v((3, 4, 512, 128), bf16),
        v((3, 4, 512, 128), bf16),
        v((16, 3, 128, 128), bf16),
        v((16, 256, 256), f32),
        v((16, 128, 512), bf16),
        v((16, 128, 128), f32),
        v((16, 128, 128), f32),
        v((16, 128, 128), bf16),
        v((4, 128, 128), bf16),
        v((4, 512, 128), bf16),
        v((4, 512, 128), bf16),
        v((4, 128, 128), bf16),
        v((2, 4, 512, 128), bf16),
        v((2, 4, 512, 128), bf16),
        v((128, 128), f32),
        v((128, 128), f32),
        v((32, 4, 128), f32),
        v((32, 4, 128), f32),
        v((128, 128), f32),
        v((128, 128), f32),
        v((32, 4, 128), f32),
        v((32, 4, 128), f32),
        v((512, 128), f32),
        v((4, 128, 256), f32),
        v((3, 4, 64, 128), bf16),
        v((3, 4, 64, 128), bf16),
        v((3, 128, 256), bf16),
        v((3, 128, 256), bf16),
        dma((5,)),
        dma((3,)), dma((3,)),
        dma((4, 4)), dma((4, 4)),
        dma((4,)), dma((4,)),
        dma((2,)), dma((2,)),
        dma((6,)), dma((6,)),
        dma((1,)), dma((1,)),
        dma((1,)), dma((1,)),
        dma((3, 4)), dma((3, 4)),
        dma((3,)), dma((3,)),
    ]
    return pl.pallas_call(
        kernel,
        out_shape=(jax.ShapeDtypeStruct((128, 256), f32), jax.ShapeDtypeStruct((128, 256), f32)),
        in_specs=[hbm] * 5,
        out_specs=(vmem, vmem),
        scratch_shapes=scratch,
        compiler_params=pltpu.CompilerParams(
            collective_id=0, has_side_effects=True, vmem_limit_bytes=60 * 1024 * 1024
        ),
    )(tokens, key_weight, value_weight, buckets[..., 0], cotangent)


def solution(mesh):
    in_specs = (
        P("seq", "head"),
        P(None, "head"),
        P(None, "head"),
        P(None, "head", "seq", None),
        P("seq", "head"),
    )
    out_specs = (P("seq", "head"), P("seq", "head"))
    return jax.shard_map(shards, mesh=mesh, in_specs=in_specs, out_specs=out_specs, check_vma=False)
```

```python
import jax
import jax.numpy as jnp
from jax import lax
from jax.experimental import pallas as pl
from jax.experimental.pallas import tpu as pltpu

P = jax.sharding.PartitionSpec
MESH = pl.DeviceIdType.MESH
f32, bf16, i32 = jnp.float32, jnp.bfloat16, jnp.int32

SHARP = 16.0
EMPTY = 1024.0
PEERS = 32
ROUNDS = 4
GROUP = 4


def iota(shape, dim):
    return lax.broadcasted_iota(i32, shape, dim)


def low_lanes(shape):
    return iota(shape, 1) % 128 < 64


def swap(x):
    return pltpu.roll(x, 64, 1)


def mm(a, b):
    return lax.dot_general(a, b, (((1,), (0,)), ((), ())), preferred_element_type=f32)


def mm_t(a, b):
    return lax.dot_general(a, b, (((1,), (1,)), ((), ())), preferred_element_type=f32)


def split2(x):
    high = x.astype(bf16)
    return high, (x - high.astype(f32)).astype(bf16)


def rank_codes(ids):
    rows = jnp.concatenate([ids[r].astype(f32) for r in range(ROUNDS)], axis=0)
    columns = jnp.concatenate([rows, jnp.zeros((112, 128), f32)], axis=0).T
    before = iota((128, 128), 0) < iota((128, 128), 1)
    codes = []
    for k in range(GROUP):
        code = jnp.zeros((8, 128), f32)
        for r in range(ROUNDS):
            at = 4 * r + k
            same = (columns[:, at : at + 1] == rows[at : at + 1, :]) & before
            rank = jnp.sum(jnp.where(same, 1.0, 0.0), axis=0, keepdims=True)
            code = jnp.where(iota((8, 128), 0) == r, rows[at : at + 1, :] + 128.0 * rank, code)
        codes.append(code.astype(i32))
    return codes


def places(codes):
    bucket, rank = codes & 127, codes >> 7
    block = iota((8, 512), 1) >> 7
    slot = bucket * 4 + block
    both = jnp.concatenate([slot[:4].astype(f32), rank[:4].astype(f32)], axis=0)
    columns = []
    for m in range(GROUP):
        tile = both[:, 128 * m : 128 * m + 128]
        columns.append(jnp.concatenate([tile, jnp.zeros((120, 128), f32)], axis=0).T)
    return bucket, rank, slot, jnp.concatenate(columns, axis=0)


def slot_onehot(slot_row):
    return jnp.where(iota((512, 512), 0) == slot_row, 1.0, 0.0).astype(bf16)


def token_onehot(slot_column):
    return jnp.where(iota((512, 512), 1).astype(f32) == slot_column, 1.0, 0.0).astype(bf16)


def half_mask(rank_column):
    half = (iota((512, 128), 1) >> 6).astype(f32)
    return jnp.where(half == rank_column, 1.0, 0.0).astype(bf16)


def halves(tile):
    top, bottom = tile[:64], tile[64:]
    low = low_lanes((64, 128))
    return jnp.where(low, top, swap(bottom)).astype(bf16), jnp.where(low, swap(top), bottom).astype(bf16)


def pack_cot(onehot, rows, mask):
    out = mm(onehot, jnp.concatenate([rows * mask, mask], axis=1))
    return jnp.where(out[:, 128:256] > 0.5, out[:, 0:128], EMPTY).astype(bf16)


def pack(onehot, rows, mask):
    return mm(onehot, rows * mask).astype(bf16)


def regroup():
    p, c = iota((128, 128), 0), iota((128, 128), 1)
    hit = ((c >> 4) == ((p & 31) >> 2)) & (((c & 15) >> 2) == (p >> 5)) & ((c & 3) == (p & 3))
    return jnp.where(hit, 1.0, 0.0).astype(bf16)


def regroup_back():
    c, p = iota((128, 128), 0), iota((128, 128), 1)
    hit = ((c >> 4) == ((p & 31) >> 2)) & (((c & 15) >> 2) == (p >> 5)) & ((c & 3) == (p & 3))
    return jnp.where(hit, 1.0, 0.0).astype(bf16)


def half_ones():
    r, c = iota((256, 128), 0), iota((256, 128), 1)
    return jnp.where(((r & 127) >> 6) == (c >> 6), 1.0, 0.0).astype(bf16)


def half_sums(x, ones):
    high, low = split2(x)
    return mm(jnp.concatenate([high, low], axis=1), ones)


def on_rows(x):
    return jnp.concatenate([x, swap(x)], axis=0)


def on_rows_low(x):
    low = low_lanes(x.shape)
    return jnp.concatenate([jnp.where(low, x, 0.0), jnp.where(low, swap(x), 0.0)], axis=0)


def on_diagonal(x):
    low, turned = low_lanes(x.shape), swap(x)
    return jnp.concatenate(
        [jnp.where(low, x, 0.0), jnp.where(low, turned, 0.0), jnp.where(low, 0.0, turned), jnp.where(low, 0.0, x)],
        axis=0,
    ).astype(bf16)


def side_by_side(x):
    return jnp.concatenate([x[:128], x[128:]], axis=1)


def diagonal():
    return iota((256, 256), 0) == iota((256, 256), 1)


def owner_scores(shared, cot, ones):
    shared = shared.astype(f32)
    scale = lax.rsqrt(half_sums(shared * shared, ones) + 1e-6)
    unit = shared * scale
    scores = mm_t(on_rows_low(unit).astype(bf16), on_rows(unit).astype(bf16))
    weights = jnp.where(diagonal(), 1.0, jnp.exp(SHARP * scores))
    low = low_lanes((128, 128))
    valid = jnp.where(cot.astype(f32) < 0.5 * EMPTY, 1.0, 0.0)
    turned = swap(valid)
    valid = jnp.concatenate([jnp.where(low, valid, turned), jnp.where(low, turned, valid)], axis=0)
    totals = jnp.sum(weights * jnp.concatenate([valid, valid], axis=1), axis=0, keepdims=True)
    return weights, side_by_side(weights.astype(bf16)), unit, scale, totals


def owner_outputs(weights, beside, values, cot):
    values, cot = values.astype(f32), cot.astype(f32)
    along = mm_t(on_rows_low(values).astype(bf16), on_rows(cot).astype(bf16))
    products = jnp.sum(weights * along, axis=0, keepdims=True)
    return mm(beside, on_diagonal(values)).astype(bf16), products


def owner_values(beside, cot, columns):
    wide = [jnp.broadcast_to(c, (128, 128)) for c in columns]
    grad_round = jnp.where(low_lanes((128, 128)), wide[0], wide[1]) * cot.astype(f32)
    return mm(beside, on_diagonal(grad_round)).astype(bf16), grad_round.astype(bf16)


def owner_shared(weights, unit, scale, values, grad_round, row, columns, ones):
    low = low_lanes((128, 128))
    wide = jnp.concatenate([jnp.broadcast_to(c, (128, 128)) for c in columns], axis=0)
    values, grad_round = values.astype(f32), grad_round.astype(f32)
    values_turned, grad_turned = swap(values), swap(grad_round)
    left = jnp.concatenate([jnp.where(low, grad_round, values_turned), jnp.where(low, grad_turned, values)], axis=0)
    right = jnp.concatenate([jnp.where(low, values, grad_turned), jnp.where(low, values_turned, grad_round)], axis=0)
    inner = mm_t(left.astype(bf16), right.astype(bf16)) - row - jnp.concatenate([wide, wide], axis=1)
    grad = jnp.where(diagonal(), 0.0, weights * inner).astype(bf16)
    grad_unit = SHARP * mm(side_by_side(grad), on_diagonal(unit))
    return ((grad_unit - unit * half_sums(unit * grad_unit, ones)) * scale).astype(bf16)


def own_tile(first, second):
    first, second = first.astype(f32), second.astype(f32)
    low = low_lanes((64, 128))
    return jnp.concatenate([jnp.where(low, first, swap(second)), jnp.where(low, swap(first), second)], axis=0)


def square(x):
    return jnp.concatenate([x, jnp.zeros((128 - x.shape[0], 128), f32)], axis=0)


def place_onehot(bucket_row, block_row):
    return jnp.where(iota((128, 512), 0) == (bucket_row >> 2) * 4 + block_row, 1.0, 0.0).astype(bf16)


def token_scalars(turned, bucket, rank):
    block = iota((1, 512), 1) >> 7
    total, product = jnp.zeros((1, 512), f32), jnp.zeros((1, 512), f32)
    for r in range(ROUNDS):
        onehot = place_onehot(bucket[r : r + 1], block)
        high, low = split2(turned[16 * r : 16 * r + 16])
        picked = mm(jnp.concatenate([high, low], axis=1), jnp.concatenate([onehot, onehot], axis=0))
        hit = iota((8, 512), 0) == rank[r : r + 1] * 4 + (bucket[r : r + 1] & 3)
        total = total + jnp.sum(jnp.where(hit, picked[0:8], 0.0), axis=0, keepdims=True)
        product = product + jnp.sum(jnp.where(hit, picked[8:16], 0.0), axis=0, keepdims=True)
    inverse = 1.0 / total
    return inverse, product * inverse * inverse


def spread_scalars(inverse, along, bucket, rank):
    block = iota((1, 512), 1) >> 7
    out = []
    for r in range(ROUNDS):
        onehot = place_onehot(bucket[r : r + 1], block)
        hit = iota((8, 512), 0) == rank[r : r + 1] * 4 + (bucket[r : r + 1] & 3)
        left = jnp.concatenate([jnp.where(hit, inverse, 0.0), jnp.where(hit, along, 0.0)], axis=0)
        high, low = split2(left)
        both = mm_t(jnp.concatenate([high, low], axis=0), onehot)
        out.append(both[0:16] + both[16:32])
    return square(jnp.concatenate(out, axis=0))


def kernel(
    tok, key_hbm, value_hbm, ids_hbm, cot_hbm, att_out, gin_out,
    gat, kw, vw, ids, cot, row_send, code_send, row_land, code_land,
    onehot, onehot_t, masks, rows_x, slots_out, slots_in, tasks,
    w_keep, beside_keep, unit_keep, scale_keep, round_keep,
    num_task, num_out, num_in, grad_task, grad_out, grad_in,
    z_rows, z_turn, z_out, z_in, q_turn, q_cols, q_out, q_in, acc, part,
    back_send, back_land, rs_send, rs_land,
    ld, s0, r0, s1, r1, s2, r2, sn, rn, sg, rg, s3, r3, s4, r4, s6, r6, s7, r7,
):
    seq, y = lax.axis_index("seq"), lax.axis_index("head")
    z, xc = lax.div(seq, 8), lax.rem(seq, 8)
    zq, zr = lax.div(z, 4), lax.rem(z, 4)
    me = xc * 4 + y
    rows = [lax.rem(y + o, 4) for o in range(4)]

    loads = ((ids_hbm, ids), (cot_hbm, cot), (tok, gat.at[y]), (key_hbm, kw), (value_hbm, vw))
    for i, (src, dst) in enumerate(loads):
        pltpu.make_async_copy(src, dst, ld.at[i]).start()

    def loaded(i):
        pltpu.make_async_copy(loads[i][0], loads[i][1], ld.at[i]).wait()

    def slab(d):
        return (z * 8 + lax.div(d, 4), lax.rem(d, 4))

    first = z < 4
    turn = jnp.where(first, 0, lax.rem(z + 2, 3) + 1)
    block = jnp.where(first, z, lax.div(z + 2, 3) - 2)
    alone = first & (z == y)

    def head_place(i):
        return ((4 * i + y) * 8 + xc, lax.rem(turn + y, 4))

    def block_home(i):
        back = lax.rem(y + 4 - zr, 4)
        return (jnp.where(back == 0, i, 3 + 3 * i + back) * 8 + xc, zr)

    def arrived(ref, sem):
        pltpu.make_async_copy(ref, ref, sem).wait()

    to_head = (head_place, block, lambda i: alone & (zq == i))
    to_home = (block_home, zq, lambda i: alone & (zr == i))

    def to_partner(way, i, src, land, send_sem, recv_sem):
        partner, slot, itself = way

        @pl.when(itself(i))
        def _():
            pltpu.make_async_copy(src, land.at[slot], recv_sem.at[slot]).start()

        @pl.when(jnp.logical_not(itself(i)))
        def _():
            pltpu.make_async_remote_copy(
                src, land.at[slot], send_sem.at[i], recv_sem.at[slot], device_id=partner(i), device_id_type=MESH
            ).start()

    def partner_sent(way, i, src, send_sem):
        @pl.when(jnp.logical_not(way[2](i)))
        def _():
            arrived(src, send_sem.at[i])

    def to_slab(out_at, in_at, send_sem, recv_sem):
        pltpu.make_async_copy(out_at(me), in_at(me), recv_sem).start()

        def start(column, row):
            d = column * 4 + row
            pltpu.make_async_remote_copy(
                out_at(d), in_at(me), send_sem, recv_sem, device_id=(z * 8 + column, row), device_id_type=MESH
            ).start()

        def send(o, carry):
            column = lax.rem(xc + o, 8)
            for row in rows:
                start(column, row)
            return carry

        for row in rows[1:]:
            start(xc, row)
        lax.fori_loop(1, 8, send, 0)

    barrier = pltpu.get_barrier_semaphore()

    def greet(o, carry):
        pl.semaphore_signal(barrier, 1, device_id=slab(lax.rem(me + o, PEERS)), device_id_type=MESH)
        return carry

    lax.fori_loop(1, PEERS, greet, 0)
    for i in range(GROUP):

        for way in (to_head, to_home):

            @pl.when(jnp.logical_not(way[2](i)))
            def _(i=i, way=way):
                pl.semaphore_signal(barrier, 1, device_id=way[0](i), device_id_type=MESH)

    loaded(0)
    for k, code in enumerate(rank_codes([ids[r] for r in range(ROUNDS)])):
        code_send[k] = code
    loaded(1)
    low64 = low_lanes((64, 128))
    for k in range(0, GROUP, 2):
        row_send[2, k], row_send[2, k + 1] = halves(cot[:, 64 * k : 64 * k + 128].astype(f32))

    pl.semaphore_wait(barrier, jnp.where(alone, 37, 39))

    for k in range(GROUP):
        to_partner(to_head, k, code_send.at[k], code_land, s1.at[0], r1.at[0])
    for o in range(1, 4):
        pltpu.make_async_remote_copy(
            tok, gat.at[y], s0.at[o - 1], r0.at[o - 1], device_id=(seq, lax.rem(y + o, 4)), device_id_type=MESH
        ).start()
    for k in range(GROUP):
        to_partner(to_head, k, row_send.at[2, k], row_land.at[2], s1.at[3], r1.at[3])

    for i in (2, 3, 4):
        loaded(i)
    for a, weight in enumerate((kw, vw)):
        result = mm(gat[y], weight[pl.ds(pl.multiple_of(y * 256, 256), 256), :])
        for o in range(1, 4):
            source = lax.rem(y + 4 - o, 4)
            if a == 0:
                arrived(gat.at[source], r0.at[o - 1])
            result = result + mm(gat[source], weight[pl.ds(pl.multiple_of(source * 256, 256), 256), :])
        for k in range(0, GROUP, 2):
            row_send[a, k], row_send[a, k + 1] = halves(result[:, 64 * k : 64 * k + 128])
        for k in range(GROUP):
            to_partner(to_head, k, row_send.at[a, k], row_land.at[a], s1.at[a + 1], r1.at[a + 1])

    for m in range(GROUP):
        arrived(code_land.at[m], r1.at[0, m])
    codes = jnp.concatenate([code_land[m] for m in range(GROUP)], axis=1)
    bucket, rank, slot, columns = places(codes)
    for r in range(ROUNDS):
        onehot[r] = slot_onehot(slot[r : r + 1])
        masks[r] = half_mask(columns[:, 4 + r : 5 + r])

    def piece(d):
        return pl.ds(pl.multiple_of(d * 16, 16), 16)

    def spread(a):
        for m in range(GROUP):
            arrived(row_land.at[a, m], r1.at[a + 1, m])
            landed = row_land[a, m].astype(f32)
            turned = swap(landed)
            rows_x[a, 128 * m : 128 * m + 64, :] = jnp.where(low64, landed, turned).astype(bf16)
            rows_x[a, 128 * m + 64 : 128 * m + 128, :] = jnp.where(low64, turned, landed).astype(bf16)

    spread(2)

    def pack_cots(r, carry):
        slots_out[2, r] = pack_cot(onehot[r], rows_x[2], masks[r])
        return carry

    lax.fori_loop(0, ROUNDS, pack_cots, 0)
    to_slab(lambda d: slots_out.at[2, :, piece(d), :], lambda d: slots_in.at[2, :, piece(d), :], s2.at[3], r2.at[3])

    spread(0)

    def pack_shared(r, carry):
        slots_out[0, r] = pack(onehot[r], rows_x[0], masks[r])
        return carry

    lax.fori_loop(0, ROUNDS, pack_shared, 0)
    to_slab(lambda d: slots_out.at[0, :, piece(d), :], lambda d: slots_in.at[0, :, piece(d), :], s2.at[0], r2.at[0])
    spread(1)

    def pack_values(p, carry):
        for i in range(2):
            slots_out[1, 2 * p + i] = pack(onehot[2 * p + i], rows_x[1], masks[2 * p + i])
        two = pl.ds(2 * p, 2)
        to_slab(
            lambda d: slots_out.at[1, two, piece(d), :],
            lambda d: slots_in.at[1, two, piece(d), :],
            s2.at[p + 1],
            r2.at[p + 1],
        )
        return carry

    lax.fori_loop(0, 2, pack_values, 0)

    for r in range(ROUNDS):
        onehot_t[r] = token_onehot(columns[:, r : r + 1])

    ones = half_ones()
    sort, unsort = regroup(), regroup_back()
    z_rows[...] = jnp.zeros((128, 128), f32)

    def sort_rows(a, r):
        for g in range(4):
            moved = mm(sort, slots_in[a, r, 128 * g : 128 * g + 128, :]).astype(bf16)
            for b in range(GROUP):
                tasks[r * 4 + b, a, 32 * g : 32 * g + 32, :] = moved[32 * b : 32 * b + 32]

    def sort_cots(r, carry):
        sort_rows(2, r)
        return carry

    arrived(slots_in.at[2], r2.at[3])
    lax.fori_loop(0, ROUNDS, sort_cots, 0)

    def scores_round(r, carry):
        sort_rows(0, r)
        for b in range(GROUP):
            t = r * 4 + b
            weights, beside, unit, scale, totals = owner_scores(tasks[t, 0], tasks[t, 2], ones)
            w_keep[t] = weights
            beside_keep[t] = beside
            unit_keep[t] = unit
            scale_keep[t] = scale
            line = r * 16 + b
            z_rows[pl.ds(line, 1), :] = totals[:, :128]
            z_rows[pl.ds(line + 4, 1), :] = totals[:, 128:]
        return carry

    arrived(slots_in.at[0], r2.at[0])
    lax.fori_loop(0, ROUNDS, scores_round, 0)

    def outputs_round(r):
        sort_rows(1, r)
        for b in range(GROUP):
            t = r * 4 + b
            numerator, products = owner_outputs(w_keep[t], beside_keep[t], tasks[t, 1], tasks[t, 2])
            num_task[b] = numerator
            line = r * 16 + b
            z_rows[pl.ds(line + 8, 1), :] = products[:, :128]
            z_rows[pl.ds(line + 12, 1), :] = products[:, 128:]
        for g in range(4):
            moved = jnp.concatenate([num_task[b, 32 * g : 32 * g + 32, :] for b in range(GROUP)], axis=0)
            num_out[r, 128 * g : 128 * g + 128, :] = mm(unsort, moved).astype(bf16)

    def outputs_pair(p, carry):
        arrived(slots_in.at[1, pl.ds(2 * p, 2)], r2.at[p + 1])
        for i in range(2):
            outputs_round(2 * p + i)
        return carry

    lax.fori_loop(0, 2, outputs_pair, 0)

    def send_numerators(p):
        two = pl.ds(2 * p, 2)
        to_slab(lambda d: num_out.at[two, piece(d), :], lambda d: num_in.at[two, piece(d), :], sn.at[p], rn.at[p])

    z_turn[...] = z_rows[...].T
    for d in range(PEERS):
        z_out[d] = z_turn[4 * d : 4 * d + 4, :]
    to_slab(lambda d: z_out.at[d], lambda d: z_in.at[d], s3.at[0], r3.at[0])
    send_numerators(0)
    arrived(z_in, r3.at[0])
    for d in range(PEERS):
        q_turn[4 * d : 4 * d + 4, :] = z_in[d]
    inverse, along = token_scalars(q_turn[...].T, bucket, rank)
    z_turn[...] = spread_scalars(inverse, along, bucket, rank).T
    for d in range(PEERS):
        q_out[d] = z_turn[4 * d : 4 * d + 4, :]
    to_slab(lambda d: q_out.at[d], lambda d: q_in.at[d], s4.at[0], r4.at[0])
    send_numerators(1)

    def add(source, r):
        acc[...] += mm(onehot_t[r], source[r]) * masks[r].astype(f32)

    def summed(source, sems):
        acc[...] = jnp.zeros((512, 128), f32)

        def pair(p, carry):
            arrived(source.at[pl.ds(2 * p, 2)], sems.at[p])
            for i in range(2):
                add(source, 2 * p + i)
            return carry

        lax.fori_loop(0, 2, pair, 0)

    def send_back(a, scale):
        for m in range(GROUP):
            rows = acc[128 * m : 128 * m + 128, :]
            rows = rows + swap(rows)
            if scale is not None:
                rows = rows * jnp.broadcast_to(scale[:, 128 * m : 128 * m + 128], (128, 128)).T
            back_send[a, m] = jnp.where(low64, rows[:64], rows[64:]).astype(bf16)
            to_partner(to_home, m, back_send.at[a, m], back_land.at[a], s6.at[a], r6.at[a])

    def own_rows(a):
        for k in range(GROUP):
            arrived(back_land.at[a, k], r6.at[a, k])
        return [own_tile(back_land[a, k], back_land[a, k + 1]) for k in range(0, GROUP, 2)]

    arrived(q_in, r4.at[0])
    for d in range(PEERS):
        q_cols[4 * d : 4 * d + 4, :] = q_in[d]
    q_turn[...] = q_cols[...].T

    def nearby(line):
        return pltpu.roll(q_cols[...], lax.rem(128 - line, 128), 1)

    def unsort_grads(a, r):
        for g in range(4):
            moved = jnp.concatenate([grad_task[b, 32 * g : 32 * g + 32, :] for b in range(GROUP)], axis=0)
            grad_out[a, r, 128 * g : 128 * g + 128, :] = mm(unsort, moved).astype(bf16)

    def values_pair(p, carry):
        for i in range(2):
            r = 2 * p + i
            for b in range(GROUP):
                t = r * 4 + b
                near = nearby(r * 16 + b)
                grad_values, grad_round = owner_values(beside_keep[t], tasks[t, 2], [near[:, c : c + 1] for c in (0, 4)])
                round_keep[t] = grad_round
                grad_task[b] = grad_values
            unsort_grads(0, r)
        two = pl.ds(2 * p, 2)
        to_slab(
            lambda d: grad_out.at[0, two, piece(d), :], lambda d: grad_in.at[0, two, piece(d), :], sg.at[p], rg.at[p]
        )
        return carry

    lax.fori_loop(0, 2, values_pair, 0)
    summed(num_in, rn)
    send_back(0, inverse)

    def shared_round(r, carry):
        for b in range(GROUP):
            t = r * 4 + b
            line = r * 16 + b
            near = nearby(line)
            row = jnp.concatenate([q_turn[pl.ds(line + 8, 1), :], q_turn[pl.ds(line + 12, 1), :]], axis=1)
            grad_task[b] = owner_shared(
                w_keep[t], unit_keep[t], scale_keep[t], tasks[t, 1], round_keep[t], row,
                [near[:, c : c + 1] for c in (8, 12)], ones,
            )
        unsort_grads(1, r)
        to_slab(
            lambda d: grad_out.at[1, r, piece(d), :], lambda d: grad_in.at[1, r, piece(d), :], sg.at[r + 2], rg.at[r + 2]
        )
        return carry

    lax.fori_loop(0, ROUNDS, shared_round, 0)

    summed(grad_in.at[0], rg)
    send_back(1, None)
    acc[...] = jnp.zeros((512, 128), f32)

    def add_shared(r, carry):
        arrived(grad_in.at[1, r], rg.at[r + 2])
        add(grad_in.at[1], r)
        return carry

    lax.fori_loop(0, ROUNDS, add_shared, 0)
    send_back(2, None)
    for k, tile in enumerate(own_rows(0)):
        att_out[:, 128 * k : 128 * k + 128] = tile

    left = jnp.concatenate(own_rows(1), axis=1).astype(bf16)
    for o in range(4):
        part[o] = mm_t(left, vw[pl.ds(pl.multiple_of(lax.rem(y + o, 4) * 256, 256), 256), :])
    left = jnp.concatenate(own_rows(2), axis=1).astype(bf16)
    for o in range(1, 4):
        d = lax.rem(y + o, 4)
        rs_send[o - 1] = (part[o] + mm_t(left, kw[pl.ds(pl.multiple_of(d * 256, 256), 256), :])).astype(bf16)
        pltpu.make_async_remote_copy(
            rs_send.at[o - 1], rs_land.at[o - 1], s7.at[o - 1], r7.at[o - 1], device_id=(seq, d), device_id_type=MESH
        ).start()
    total = part[0] + mm_t(left, kw[pl.ds(pl.multiple_of(y * 256, 256), 256), :])
    for o in range(1, 4):
        arrived(rs_land.at[o - 1], r7.at[o - 1])
        total = total + rs_land[o - 1].astype(f32)
    gin_out[...] = total

    for o in range(3):
        arrived(gat.at[o], s0.at[o])
        arrived(rs_send.at[o], s7.at[o])
    for k in range(GROUP):
        partner_sent(to_head, k, code_send.at[k], s1.at[0])
        for a in range(3):
            partner_sent(to_head, k, row_send.at[a, k], s1.at[a + 1])
            partner_sent(to_home, k, back_send.at[a, k], s6.at[a])
    rest = pl.ds(0, 16 * (PEERS - 1))
    arrived(slots_out.at[0, :, rest, :], s2.at[0])
    arrived(slots_out.at[2, :, rest, :], s2.at[3])
    for p in range(2):
        two = pl.ds(2 * p, 2)
        arrived(slots_out.at[1, two, rest, :], s2.at[p + 1])
        arrived(num_out.at[two, rest, :], sn.at[p])
        arrived(grad_out.at[0, two, rest, :], sg.at[p])
    for r in range(ROUNDS):
        arrived(grad_out.at[1, r, rest, :], sg.at[r + 2])
    arrived(z_out.at[pl.ds(0, PEERS - 1)], s3.at[0])
    arrived(q_out.at[pl.ds(0, PEERS - 1)], s4.at[0])


def shards(tokens, key_weight, value_weight, buckets, cotangent):
    vmem, hbm = pl.BlockSpec(memory_space=pltpu.VMEM), pl.BlockSpec(memory_space=pl.ANY)
    v, dma = pltpu.VMEM, pltpu.SemaphoreType.DMA
    scratch = [
        v((4, 128, 256), bf16),
        v((1024, 256), bf16),
        v((1024, 256), bf16),
        v((4, 4, 128), i32),
        v((128, 256), bf16),
        v((3, 4, 64, 128), bf16),
        v((4, 8, 128), i32),
        v((3, 4, 64, 128), bf16),
        v((4, 8, 128), i32),
        v((4, 512, 512), bf16),
        v((4, 512, 512), bf16),
        v((4, 512, 128), bf16),
        v((3, 512, 128), bf16),
        v((3, 4, 512, 128), bf16),
        v((3, 4, 512, 128), bf16),
        v((16, 3, 128, 128), bf16),
        v((16, 256, 256), f32),
        v((16, 128, 512), bf16),
        v((16, 128, 128), f32),
        v((16, 128, 128), f32),
        v((16, 128, 128), bf16),
        v((4, 128, 128), bf16),
        v((4, 512, 128), bf16),
        v((4, 512, 128), bf16),
        v((4, 128, 128), bf16),
        v((2, 4, 512, 128), bf16),
        v((2, 4, 512, 128), bf16),
        v((128, 128), f32),
        v((128, 128), f32),
        v((32, 4, 128), f32),
        v((32, 4, 128), f32),
        v((128, 128), f32),
        v((128, 128), f32),
        v((32, 4, 128), f32),
        v((32, 4, 128), f32),
        v((512, 128), f32),
        v((4, 128, 256), f32),
        v((3, 4, 64, 128), bf16),
        v((3, 4, 64, 128), bf16),
        v((3, 128, 256), bf16),
        v((3, 128, 256), bf16),
        dma((5,)),
        dma((3,)), dma((3,)),
        dma((4, 4)), dma((4, 4)),
        dma((4,)), dma((4,)),
        dma((2,)), dma((2,)),
        dma((6,)), dma((6,)),
        dma((1,)), dma((1,)),
        dma((1,)), dma((1,)),
        dma((3, 4)), dma((3, 4)),
        dma((3,)), dma((3,)),
    ]
    return pl.pallas_call(
        kernel,
        out_shape=(jax.ShapeDtypeStruct((128, 256), f32), jax.ShapeDtypeStruct((128, 256), f32)),
        in_specs=[hbm] * 5,
        out_specs=(vmem, vmem),
        scratch_shapes=scratch,
        compiler_params=pltpu.CompilerParams(
            collective_id=0, has_side_effects=True, vmem_limit_bytes=60 * 1024 * 1024
        ),
    )(tokens, key_weight, value_weight, buckets[..., 0], cotangent)


def solution(mesh):
    in_specs = (
        P("seq", "head"),
        P(None, "head"),
        P(None, "head"),
        P(None, "head", "seq", None),
        P("seq", "head"),
    )
    out_specs = (P("seq", "head"), P("seq", "head"))
    return jax.shard_map(shards, mesh=mesh, in_specs=in_specs, out_specs=out_specs, check_vma=False)
```

```python
import jax
import jax.numpy as jnp
from jax import lax
from jax.experimental import pallas as pl
from jax.experimental.pallas import tpu as pltpu

P = jax.sharding.PartitionSpec
MESH = pl.DeviceIdType.MESH
f32, bf16, i32 = jnp.float32, jnp.bfloat16, jnp.int32

SHARP = 16.0
EMPTY = 1024.0
PEERS = 32
ROUNDS = 4
GROUP = 4


def iota(shape, dim):
    return lax.broadcasted_iota(i32, shape, dim)


def low_lanes(shape):
    return iota(shape, 1) % 128 < 64


def swap(x):
    return pltpu.roll(x, 64, 1)


def mm(a, b):
    return lax.dot_general(a, b, (((1,), (0,)), ((), ())), preferred_element_type=f32)


def mm_t(a, b):
    return lax.dot_general(a, b, (((1,), (1,)), ((), ())), preferred_element_type=f32)


def split2(x):
    high = x.astype(bf16)
    return high, (x - high.astype(f32)).astype(bf16)


def rank_codes(ids):
    rows = jnp.concatenate([ids[r].astype(f32) for r in range(ROUNDS)], axis=0)
    columns = jnp.concatenate([rows, jnp.zeros((112, 128), f32)], axis=0).T
    before = iota((128, 128), 0) < iota((128, 128), 1)
    codes = []
    for k in range(GROUP):
        code = jnp.zeros((8, 128), f32)
        for r in range(ROUNDS):
            at = 4 * r + k
            same = (columns[:, at : at + 1] == rows[at : at + 1, :]) & before
            rank = jnp.sum(jnp.where(same, 1.0, 0.0), axis=0, keepdims=True)
            code = jnp.where(iota((8, 128), 0) == r, rows[at : at + 1, :] + 128.0 * rank, code)
        codes.append(code.astype(i32))
    return codes


def places(codes):
    bucket, rank = codes & 127, codes >> 7
    block = iota((8, 512), 1) >> 7
    slot = bucket * 4 + block
    both = jnp.concatenate([slot[:4].astype(f32), rank[:4].astype(f32)], axis=0)
    columns = []
    for m in range(GROUP):
        tile = both[:, 128 * m : 128 * m + 128]
        columns.append(jnp.concatenate([tile, jnp.zeros((120, 128), f32)], axis=0).T)
    return bucket, rank, slot, jnp.concatenate(columns, axis=0)


def slot_onehot(slot_row):
    return jnp.where(iota((512, 512), 0) == slot_row, 1.0, 0.0).astype(bf16)


def token_onehot(slot_column):
    return jnp.where(iota((512, 512), 1).astype(f32) == slot_column, 1.0, 0.0).astype(bf16)


def half_mask(rank_column):
    half = (iota((512, 128), 1) >> 6).astype(f32)
    return jnp.where(half == rank_column, 1.0, 0.0).astype(bf16)


def halves(tile):
    top, bottom = tile[:64], tile[64:]
    low = low_lanes((64, 128))
    return jnp.where(low, top, swap(bottom)).astype(bf16), jnp.where(low, swap(top), bottom).astype(bf16)


def pack_cot(onehot, rows, mask):
    out = mm(onehot, jnp.concatenate([rows * mask, mask], axis=1))
    return jnp.where(out[:, 128:256] > 0.5, out[:, 0:128], EMPTY).astype(bf16)


def pack(onehot, rows, mask):
    return mm(onehot, rows * mask).astype(bf16)


def regroup():
    p, c = iota((128, 128), 0), iota((128, 128), 1)
    hit = ((c >> 4) == ((p & 31) >> 2)) & (((c & 15) >> 2) == (p >> 5)) & ((c & 3) == (p & 3))
    return jnp.where(hit, 1.0, 0.0).astype(bf16)


def regroup_back():
    c, p = iota((128, 128), 0), iota((128, 128), 1)
    hit = ((c >> 4) == ((p & 31) >> 2)) & (((c & 15) >> 2) == (p >> 5)) & ((c & 3) == (p & 3))
    return jnp.where(hit, 1.0, 0.0).astype(bf16)


def half_ones():
    r, c = iota((256, 128), 0), iota((256, 128), 1)
    return jnp.where(((r & 127) >> 6) == (c >> 6), 1.0, 0.0).astype(bf16)


def half_sums(x, ones):
    high, low = split2(x)
    return mm(jnp.concatenate([high, low], axis=1), ones)


def on_rows(x):
    return jnp.concatenate([x, swap(x)], axis=0)


def on_rows_low(x):
    low = low_lanes(x.shape)
    return jnp.concatenate([jnp.where(low, x, 0.0), jnp.where(low, swap(x), 0.0)], axis=0)


def on_diagonal(x):
    low, turned = low_lanes(x.shape), swap(x)
    return jnp.concatenate(
        [jnp.where(low, x, 0.0), jnp.where(low, turned, 0.0), jnp.where(low, 0.0, turned), jnp.where(low, 0.0, x)],
        axis=0,
    ).astype(bf16)


def side_by_side(x):
    return jnp.concatenate([x[:128], x[128:]], axis=1)


def diagonal():
    return iota((256, 256), 0) == iota((256, 256), 1)


def owner_scores(shared, cot, ones):
    shared = shared.astype(f32)
    scale = lax.rsqrt(half_sums(shared * shared, ones) + 1e-6)
    unit = shared * scale
    scores = mm_t(on_rows_low(unit).astype(bf16), on_rows(unit).astype(bf16))
    weights = jnp.where(diagonal(), 1.0, jnp.exp(SHARP * scores))
    low = low_lanes((128, 128))
    valid = jnp.where(cot.astype(f32) < 0.5 * EMPTY, 1.0, 0.0)
    turned = swap(valid)
    valid = jnp.concatenate([jnp.where(low, valid, turned), jnp.where(low, turned, valid)], axis=0)
    totals = jnp.sum(weights * jnp.concatenate([valid, valid], axis=1), axis=0, keepdims=True)
    return weights, side_by_side(weights.astype(bf16)), unit, scale, totals


def owner_outputs(weights, beside, values, cot):
    values, cot = values.astype(f32), cot.astype(f32)
    along = mm_t(on_rows_low(values).astype(bf16), on_rows(cot).astype(bf16))
    products = jnp.sum(weights * along, axis=0, keepdims=True)
    return mm(beside, on_diagonal(values)).astype(bf16), products


def owner_values(beside, cot, columns):
    wide = [jnp.broadcast_to(c, (128, 128)) for c in columns]
    grad_round = jnp.where(low_lanes((128, 128)), wide[0], wide[1]) * cot.astype(f32)
    return mm(beside, on_diagonal(grad_round)).astype(bf16), grad_round.astype(bf16)


def owner_shared(weights, unit, scale, values, grad_round, row, columns, ones):
    low = low_lanes((128, 128))
    wide = jnp.concatenate([jnp.broadcast_to(c, (128, 128)) for c in columns], axis=0)
    values, grad_round = values.astype(f32), grad_round.astype(f32)
    values_turned, grad_turned = swap(values), swap(grad_round)
    left = jnp.concatenate([jnp.where(low, grad_round, values_turned), jnp.where(low, grad_turned, values)], axis=0)
    right = jnp.concatenate([jnp.where(low, values, grad_turned), jnp.where(low, values_turned, grad_round)], axis=0)
    inner = mm_t(left.astype(bf16), right.astype(bf16)) - row - jnp.concatenate([wide, wide], axis=1)
    grad = jnp.where(diagonal(), 0.0, weights * inner).astype(bf16)
    grad_unit = SHARP * mm(side_by_side(grad), on_diagonal(unit))
    return ((grad_unit - unit * half_sums(unit * grad_unit, ones)) * scale).astype(bf16)


def own_tile(first, second):
    first, second = first.astype(f32), second.astype(f32)
    low = low_lanes((64, 128))
    return jnp.concatenate([jnp.where(low, first, swap(second)), jnp.where(low, swap(first), second)], axis=0)


def square(x):
    return jnp.concatenate([x, jnp.zeros((128 - x.shape[0], 128), f32)], axis=0)


def place_onehot(bucket_row, block_row):
    return jnp.where(iota((128, 512), 0) == (bucket_row >> 2) * 4 + block_row, 1.0, 0.0).astype(bf16)


def token_scalars(turned, bucket, rank):
    block = iota((1, 512), 1) >> 7
    total, product = jnp.zeros((1, 512), f32), jnp.zeros((1, 512), f32)
    for r in range(ROUNDS):
        onehot = place_onehot(bucket[r : r + 1], block)
        high, low = split2(turned[16 * r : 16 * r + 16])
        picked = mm(jnp.concatenate([high, low], axis=1), jnp.concatenate([onehot, onehot], axis=0))
        hit = iota((8, 512), 0) == rank[r : r + 1] * 4 + (bucket[r : r + 1] & 3)
        total = total + jnp.sum(jnp.where(hit, picked[0:8], 0.0), axis=0, keepdims=True)
        product = product + jnp.sum(jnp.where(hit, picked[8:16], 0.0), axis=0, keepdims=True)
    inverse = 1.0 / total
    return inverse, product * inverse * inverse


def spread_scalars(inverse, along, bucket, rank):
    block = iota((1, 512), 1) >> 7
    out = []
    for r in range(ROUNDS):
        onehot = place_onehot(bucket[r : r + 1], block)
        hit = iota((8, 512), 0) == rank[r : r + 1] * 4 + (bucket[r : r + 1] & 3)
        left = jnp.concatenate([jnp.where(hit, inverse, 0.0), jnp.where(hit, along, 0.0)], axis=0)
        high, low = split2(left)
        both = mm_t(jnp.concatenate([high, low], axis=0), onehot)
        out.append(both[0:16] + both[16:32])
    return square(jnp.concatenate(out, axis=0))


def kernel(
    tok, key_hbm, value_hbm, ids_hbm, cot_hbm, att_out, gin_out,
    gat, kw, vw, ids, cot, row_send, code_send, row_land, code_land,
    onehot, onehot_t, masks, rows_x, slots_out, slots_in, tasks,
    w_keep, beside_keep, unit_keep, scale_keep, round_keep,
    num_task, num_out, num_in, grad_task, grad_out, grad_in,
    z_rows, z_turn, z_out, z_in, q_turn, q_cols, q_out, q_in, acc, part,
    back_send, back_land, rs_send, rs_land,
    ld, s0, r0, s1, r1, s2, r2, sn, rn, sg, rg, s3, r3, s4, r4, s6, r6, s7, r7,
):
    seq, y = lax.axis_index("seq"), lax.axis_index("head")
    z, xc = lax.div(seq, 8), lax.rem(seq, 8)
    zq, zr = lax.div(z, 4), lax.rem(z, 4)
    me = xc * 4 + y
    rows = [lax.rem(y + o, 4) for o in range(4)]

    loads = ((ids_hbm, ids), (cot_hbm, cot), (tok, gat.at[y]), (key_hbm, kw), (value_hbm, vw))
    for i, (src, dst) in enumerate(loads):
        pltpu.make_async_copy(src, dst, ld.at[i]).start()

    def loaded(i):
        pltpu.make_async_copy(loads[i][0], loads[i][1], ld.at[i]).wait()

    def slab(d):
        return (z * 8 + lax.div(d, 4), lax.rem(d, 4))

    first = z < 4
    turn = jnp.where(first, 0, lax.rem(z + 2, 3) + 1)
    block = jnp.where(first, z, lax.div(z + 2, 3) - 2)
    alone = first & (z == y)

    def head_place(i):
        return ((4 * i + y) * 8 + xc, lax.rem(turn + y, 4))

    def block_home(i):
        back = lax.rem(y + 4 - zr, 4)
        return (jnp.where(back == 0, i, 3 + 3 * i + back) * 8 + xc, zr)

    def arrived(ref, sem):
        pltpu.make_async_copy(ref, ref, sem).wait()

    to_head = (head_place, block, lambda i: alone & (zq == i))
    to_home = (block_home, zq, lambda i: alone & (zr == i))

    def to_partner(way, i, src, land, send_sem, recv_sem):
        partner, slot, itself = way

        @pl.when(itself(i))
        def _():
            pltpu.make_async_copy(src, land.at[slot], recv_sem.at[slot]).start()

        @pl.when(jnp.logical_not(itself(i)))
        def _():
            pltpu.make_async_remote_copy(
                src, land.at[slot], send_sem.at[i], recv_sem.at[slot], device_id=partner(i), device_id_type=MESH
            ).start()

    def partner_sent(way, i, src, send_sem):
        @pl.when(jnp.logical_not(way[2](i)))
        def _():
            arrived(src, send_sem.at[i])

    def to_slab(out_at, in_at, send_sem, recv_sem):
        pltpu.make_async_copy(out_at(me), in_at(me), recv_sem).start()

        def start(column, row):
            d = column * 4 + row
            pltpu.make_async_remote_copy(
                out_at(d), in_at(me), send_sem, recv_sem, device_id=(z * 8 + column, row), device_id_type=MESH
            ).start()

        def send(o, carry):
            column = lax.rem(xc + o, 8)
            for row in rows:
                start(column, row)
            return carry

        for row in rows[1:]:
            start(xc, row)
        lax.fori_loop(1, 8, send, 0)

    barrier = pltpu.get_barrier_semaphore()

    def greet(o, carry):
        pl.semaphore_signal(barrier, 1, device_id=slab(lax.rem(me + o, PEERS)), device_id_type=MESH)
        return carry

    lax.fori_loop(1, PEERS, greet, 0)
    for i in range(GROUP):

        for way in (to_head, to_home):

            @pl.when(jnp.logical_not(way[2](i)))
            def _(i=i, way=way):
                pl.semaphore_signal(barrier, 1, device_id=way[0](i), device_id_type=MESH)

    loaded(0)
    for k, code in enumerate(rank_codes([ids[r] for r in range(ROUNDS)])):
        code_send[k] = code
    loaded(1)
    low64 = low_lanes((64, 128))
    for k in range(0, GROUP, 2):
        row_send[2, k], row_send[2, k + 1] = halves(cot[:, 64 * k : 64 * k + 128].astype(f32))

    pl.semaphore_wait(barrier, jnp.where(alone, 37, 39))

    for k in range(GROUP):
        to_partner(to_head, k, code_send.at[k], code_land, s1.at[0], r1.at[0])
    for o in range(1, 4):
        pltpu.make_async_remote_copy(
            tok, gat.at[y], s0.at[o - 1], r0.at[o - 1], device_id=(seq, lax.rem(y + o, 4)), device_id_type=MESH
        ).start()
    for k in range(GROUP):
        to_partner(to_head, k, row_send.at[2, k], row_land.at[2], s1.at[3], r1.at[3])

    for i in (2, 3, 4):
        loaded(i)
    for a, weight in enumerate((kw, vw)):
        result = mm(gat[y], weight[pl.ds(pl.multiple_of(y * 256, 256), 256), :])
        for o in range(1, 4):
            source = lax.rem(y + 4 - o, 4)
            if a == 0:
                arrived(gat.at[source], r0.at[o - 1])
            result = result + mm(gat[source], weight[pl.ds(pl.multiple_of(source * 256, 256), 256), :])
        for k in range(0, GROUP, 2):
            row_send[a, k], row_send[a, k + 1] = halves(result[:, 64 * k : 64 * k + 128])
        for k in range(GROUP):
            to_partner(to_head, k, row_send.at[a, k], row_land.at[a], s1.at[a + 1], r1.at[a + 1])

    for m in range(GROUP):
        arrived(code_land.at[m], r1.at[0, m])
    codes = jnp.concatenate([code_land[m] for m in range(GROUP)], axis=1)
    bucket, rank, slot, columns = places(codes)
    for r in range(ROUNDS):
        onehot[r] = slot_onehot(slot[r : r + 1])
        masks[r] = half_mask(columns[:, 4 + r : 5 + r])

    def piece(d):
        return pl.ds(pl.multiple_of(d * 16, 16), 16)

    def spread(a):
        for m in range(GROUP):
            arrived(row_land.at[a, m], r1.at[a + 1, m])
            landed = row_land[a, m].astype(f32)
            turned = swap(landed)
            rows_x[a, 128 * m : 128 * m + 64, :] = jnp.where(low64, landed, turned).astype(bf16)
            rows_x[a, 128 * m + 64 : 128 * m + 128, :] = jnp.where(low64, turned, landed).astype(bf16)

    spread(2)

    def pack_cots(r, carry):
        slots_out[2, r] = pack_cot(onehot[r], rows_x[2], masks[r])
        return carry

    lax.fori_loop(0, ROUNDS, pack_cots, 0)
    to_slab(lambda d: slots_out.at[2, :, piece(d), :], lambda d: slots_in.at[2, :, piece(d), :], s2.at[4], r2.at[4])

    spread(0)

    def pack_pair(a):
        def pair(p, carry):
            for i in range(2):
                slots_out[a, 2 * p + i] = pack(onehot[2 * p + i], rows_x[a], masks[2 * p + i])
            two = pl.ds(2 * p, 2)
            to_slab(
                lambda d: slots_out.at[a, two, piece(d), :],
                lambda d: slots_in.at[a, two, piece(d), :],
                s2.at[2 * a + p],
                r2.at[2 * a + p],
            )
            return carry

        return pair

    lax.fori_loop(0, 2, pack_pair(0), 0)
    spread(1)
    lax.fori_loop(0, 2, pack_pair(1), 0)

    for r in range(ROUNDS):
        onehot_t[r] = token_onehot(columns[:, r : r + 1])

    ones = half_ones()
    sort, unsort = regroup(), regroup_back()
    z_rows[...] = jnp.zeros((128, 128), f32)

    def sort_rows(a, r):
        for g in range(4):
            moved = mm(sort, slots_in[a, r, 128 * g : 128 * g + 128, :]).astype(bf16)
            for b in range(GROUP):
                tasks[r * 4 + b, a, 32 * g : 32 * g + 32, :] = moved[32 * b : 32 * b + 32]

    def sort_cots(r, carry):
        sort_rows(2, r)
        return carry

    arrived(slots_in.at[2], r2.at[4])
    lax.fori_loop(0, ROUNDS, sort_cots, 0)

    def scores_round(r, carry):
        sort_rows(0, r)
        for b in range(GROUP):
            t = r * 4 + b
            weights, beside, unit, scale, totals = owner_scores(tasks[t, 0], tasks[t, 2], ones)
            w_keep[t] = weights
            beside_keep[t] = beside
            unit_keep[t] = unit
            scale_keep[t] = scale
            line = r * 16 + b
            z_rows[pl.ds(line, 1), :] = totals[:, :128]
            z_rows[pl.ds(line + 4, 1), :] = totals[:, 128:]
        return carry

    for p in range(2):
        arrived(slots_in.at[0, pl.ds(2 * p, 2)], r2.at[p])
        lax.fori_loop(2 * p, 2 * p + 2, scores_round, 0)

    def outputs_round(r):
        sort_rows(1, r)
        for b in range(GROUP):
            t = r * 4 + b
            numerator, products = owner_outputs(w_keep[t], beside_keep[t], tasks[t, 1], tasks[t, 2])
            num_task[b] = numerator
            line = r * 16 + b
            z_rows[pl.ds(line + 8, 1), :] = products[:, :128]
            z_rows[pl.ds(line + 12, 1), :] = products[:, 128:]
        for g in range(4):
            moved = jnp.concatenate([num_task[b, 32 * g : 32 * g + 32, :] for b in range(GROUP)], axis=0)
            num_out[r, 128 * g : 128 * g + 128, :] = mm(unsort, moved).astype(bf16)

    def outputs_pair(p, carry):
        arrived(slots_in.at[1, pl.ds(2 * p, 2)], r2.at[p + 2])
        for i in range(2):
            outputs_round(2 * p + i)
        return carry

    lax.fori_loop(0, 2, outputs_pair, 0)

    def send_numerators(p):
        two = pl.ds(2 * p, 2)
        to_slab(lambda d: num_out.at[two, piece(d), :], lambda d: num_in.at[two, piece(d), :], sn.at[p], rn.at[p])

    z_turn[...] = z_rows[...].T
    for d in range(PEERS):
        z_out[d] = z_turn[4 * d : 4 * d + 4, :]
    to_slab(lambda d: z_out.at[d], lambda d: z_in.at[d], s3.at[0], r3.at[0])
    send_numerators(0)
    arrived(z_in, r3.at[0])
    for d in range(PEERS):
        q_turn[4 * d : 4 * d + 4, :] = z_in[d]
    inverse, along = token_scalars(q_turn[...].T, bucket, rank)
    z_turn[...] = spread_scalars(inverse, along, bucket, rank).T
    for d in range(PEERS):
        q_out[d] = z_turn[4 * d : 4 * d + 4, :]
    to_slab(lambda d: q_out.at[d], lambda d: q_in.at[d], s4.at[0], r4.at[0])
    send_numerators(1)

    def add(source, r):
        acc[...] += mm(onehot_t[r], source[r]) * masks[r].astype(f32)

    def summed(source, sems):
        acc[...] = jnp.zeros((512, 128), f32)

        def pair(p, carry):
            arrived(source.at[pl.ds(2 * p, 2)], sems.at[p])
            for i in range(2):
                add(source, 2 * p + i)
            return carry

        lax.fori_loop(0, 2, pair, 0)

    def send_back(a, scale):
        for m in range(GROUP):
            rows = acc[128 * m : 128 * m + 128, :]
            rows = rows + swap(rows)
            if scale is not None:
                rows = rows * jnp.broadcast_to(scale[:, 128 * m : 128 * m + 128], (128, 128)).T
            back_send[a, m] = jnp.where(low64, rows[:64], rows[64:]).astype(bf16)
            to_partner(to_home, m, back_send.at[a, m], back_land.at[a], s6.at[a], r6.at[a])

    def own_rows(a):
        for k in range(GROUP):
            arrived(back_land.at[a, k], r6.at[a, k])
        return [own_tile(back_land[a, k], back_land[a, k + 1]) for k in range(0, GROUP, 2)]

    arrived(q_in, r4.at[0])
    for d in range(PEERS):
        q_cols[4 * d : 4 * d + 4, :] = q_in[d]
    q_turn[...] = q_cols[...].T

    def nearby(line):
        return pltpu.roll(q_cols[...], lax.rem(128 - line, 128), 1)

    def unsort_grads(a, r):
        for g in range(4):
            moved = jnp.concatenate([grad_task[b, 32 * g : 32 * g + 32, :] for b in range(GROUP)], axis=0)
            grad_out[a, r, 128 * g : 128 * g + 128, :] = mm(unsort, moved).astype(bf16)

    def values_pair(p, carry):
        for i in range(2):
            r = 2 * p + i
            for b in range(GROUP):
                t = r * 4 + b
                near = nearby(r * 16 + b)
                grad_values, grad_round = owner_values(beside_keep[t], tasks[t, 2], [near[:, c : c + 1] for c in (0, 4)])
                round_keep[t] = grad_round
                grad_task[b] = grad_values
            unsort_grads(0, r)
        two = pl.ds(2 * p, 2)
        to_slab(
            lambda d: grad_out.at[0, two, piece(d), :], lambda d: grad_in.at[0, two, piece(d), :], sg.at[p], rg.at[p]
        )
        return carry

    lax.fori_loop(0, 2, values_pair, 0)
    summed(num_in, rn)
    send_back(0, inverse)

    def shared_round(r, carry):
        for b in range(GROUP):
            t = r * 4 + b
            line = r * 16 + b
            near = nearby(line)
            row = jnp.concatenate([q_turn[pl.ds(line + 8, 1), :], q_turn[pl.ds(line + 12, 1), :]], axis=1)
            grad_task[b] = owner_shared(
                w_keep[t], unit_keep[t], scale_keep[t], tasks[t, 1], round_keep[t], row,
                [near[:, c : c + 1] for c in (8, 12)], ones,
            )
        unsort_grads(1, r)
        to_slab(
            lambda d: grad_out.at[1, r, piece(d), :], lambda d: grad_in.at[1, r, piece(d), :], sg.at[r + 2], rg.at[r + 2]
        )
        return carry

    lax.fori_loop(0, ROUNDS, shared_round, 0)

    summed(grad_in.at[0], rg)
    send_back(1, None)
    acc[...] = jnp.zeros((512, 128), f32)

    def add_shared(r, carry):
        arrived(grad_in.at[1, r], rg.at[r + 2])
        add(grad_in.at[1], r)
        return carry

    lax.fori_loop(0, ROUNDS, add_shared, 0)
    send_back(2, None)
    for k, tile in enumerate(own_rows(0)):
        att_out[:, 128 * k : 128 * k + 128] = tile

    left = jnp.concatenate(own_rows(1), axis=1).astype(bf16)
    for o in range(4):
        part[o] = mm_t(left, vw[pl.ds(pl.multiple_of(lax.rem(y + o, 4) * 256, 256), 256), :])
    left = jnp.concatenate(own_rows(2), axis=1).astype(bf16)
    for o in range(1, 4):
        d = lax.rem(y + o, 4)
        rs_send[o - 1] = (part[o] + mm_t(left, kw[pl.ds(pl.multiple_of(d * 256, 256), 256), :])).astype(bf16)
        pltpu.make_async_remote_copy(
            rs_send.at[o - 1], rs_land.at[o - 1], s7.at[o - 1], r7.at[o - 1], device_id=(seq, d), device_id_type=MESH
        ).start()
    total = part[0] + mm_t(left, kw[pl.ds(pl.multiple_of(y * 256, 256), 256), :])
    for o in range(1, 4):
        arrived(rs_land.at[o - 1], r7.at[o - 1])
        total = total + rs_land[o - 1].astype(f32)
    gin_out[...] = total

    for o in range(3):
        arrived(gat.at[o], s0.at[o])
        arrived(rs_send.at[o], s7.at[o])
    for k in range(GROUP):
        partner_sent(to_head, k, code_send.at[k], s1.at[0])
        for a in range(3):
            partner_sent(to_head, k, row_send.at[a, k], s1.at[a + 1])
            partner_sent(to_home, k, back_send.at[a, k], s6.at[a])
    rest = pl.ds(0, 16 * (PEERS - 1))
    arrived(slots_out.at[2, :, rest, :], s2.at[4])
    for p in range(2):
        two = pl.ds(2 * p, 2)
        for a in range(2):
            arrived(slots_out.at[a, two, rest, :], s2.at[2 * a + p])
        arrived(num_out.at[two, rest, :], sn.at[p])
        arrived(grad_out.at[0, two, rest, :], sg.at[p])
    for r in range(ROUNDS):
        arrived(grad_out.at[1, r, rest, :], sg.at[r + 2])
    arrived(z_out.at[pl.ds(0, PEERS - 1)], s3.at[0])
    arrived(q_out.at[pl.ds(0, PEERS - 1)], s4.at[0])


def shards(tokens, key_weight, value_weight, buckets, cotangent):
    vmem, hbm = pl.BlockSpec(memory_space=pltpu.VMEM), pl.BlockSpec(memory_space=pl.ANY)
    v, dma = pltpu.VMEM, pltpu.SemaphoreType.DMA
    scratch = [
        v((4, 128, 256), bf16),
        v((1024, 256), bf16),
        v((1024, 256), bf16),
        v((4, 4, 128), i32),
        v((128, 256), bf16),
        v((3, 4, 64, 128), bf16),
        v((4, 8, 128), i32),
        v((3, 4, 64, 128), bf16),
        v((4, 8, 128), i32),
        v((4, 512, 512), bf16),
        v((4, 512, 512), bf16),
        v((4, 512, 128), bf16),
        v((3, 512, 128), bf16),
        v((3, 4, 512, 128), bf16),
        v((3, 4, 512, 128), bf16),
        v((16, 3, 128, 128), bf16),
        v((16, 256, 256), f32),
        v((16, 128, 512), bf16),
        v((16, 128, 128), f32),
        v((16, 128, 128), f32),
        v((16, 128, 128), bf16),
        v((4, 128, 128), bf16),
        v((4, 512, 128), bf16),
        v((4, 512, 128), bf16),
        v((4, 128, 128), bf16),
        v((2, 4, 512, 128), bf16),
        v((2, 4, 512, 128), bf16),
        v((128, 128), f32),
        v((128, 128), f32),
        v((32, 4, 128), f32),
        v((32, 4, 128), f32),
        v((128, 128), f32),
        v((128, 128), f32),
        v((32, 4, 128), f32),
        v((32, 4, 128), f32),
        v((512, 128), f32),
        v((4, 128, 256), f32),
        v((3, 4, 64, 128), bf16),
        v((3, 4, 64, 128), bf16),
        v((3, 128, 256), bf16),
        v((3, 128, 256), bf16),
        dma((5,)),
        dma((3,)), dma((3,)),
        dma((4, 4)), dma((4, 4)),
        dma((5,)), dma((5,)),
        dma((2,)), dma((2,)),
        dma((6,)), dma((6,)),
        dma((1,)), dma((1,)),
        dma((1,)), dma((1,)),
        dma((3, 4)), dma((3, 4)),
        dma((3,)), dma((3,)),
    ]
    return pl.pallas_call(
        kernel,
        out_shape=(jax.ShapeDtypeStruct((128, 256), f32), jax.ShapeDtypeStruct((128, 256), f32)),
        in_specs=[hbm] * 5,
        out_specs=(vmem, vmem),
        scratch_shapes=scratch,
        compiler_params=pltpu.CompilerParams(
            collective_id=0, has_side_effects=True, vmem_limit_bytes=60 * 1024 * 1024
        ),
    )(tokens, key_weight, value_weight, buckets[..., 0], cotangent)


def solution(mesh):
    in_specs = (
        P("seq", "head"),
        P(None, "head"),
        P(None, "head"),
        P(None, "head", "seq", None),
        P("seq", "head"),
    )
    out_specs = (P("seq", "head"), P("seq", "head"))
    return jax.shard_map(shards, mesh=mesh, in_specs=in_specs, out_specs=out_specs, check_vma=False)
```
